128 devices in a mesh: heads: 4 (over y_hi, core), seq: 32 (over z, x, y_lo).
Axes of the slice: x: 4, y: 4 (y_hi: 2, y_lo: 2; y = y_hi * 2 + y_lo), z: 4, core: 2. Of those that a mesh axis runs over, the one named last changes fastest.
Arguments:
- queries: bfloat16 [65536, 8, 512], P('seq', 'heads'), may hold values from -6 to 6
- key_rows: bfloat16 [65536, 8, 512], P('seq', 'heads'), may hold values from -6 to 6
- value_rows: bfloat16 [65536, 8, 512], P('seq', 'heads'), may hold values from -6 to 6
- step_rates: bfloat16 [8, 65536], P('heads', 'seq'), may hold values from 0.25 to 4
- live_counts: int32 [32], replicated, may hold values from 256 to 2048, as said below
- group_scales: float32 [8], P('heads'), may hold values from 0.4 to 1.8
- w_first: float32 [8, 512, 512], P('heads', 'seq'), may hold values from -0.8838835 to 0.8838835
- w_third: float32 [8, 512, 512], P('heads', 'seq'), may hold values from -0.8838835 to 0.8838835
- w_second: float32 [8, 512, 512], P('heads', 'seq'), may hold values from -0.8838835 to 0.8838835
Outputs:
- fast_out: bfloat16 [65536, 8, 512], P('seq', 'heads')
The draws below stay inside these ranges and needn't reach their ends.
Inputs may be any that keep to these rules, and one draw needn't show every extreme that they name: `live_counts`: live token count of each clip shard; every draw has one shard of 2048 live tokens.
All inputs are finite; a program needn't handle non-finite values.
Results may differ from the reference program's by a relative error of at most 0.012.
The reference program's roundings to bfloat16 on the way count: a program that leaves them out, or rounds other values in their place, can miss the bound.
Values may be sent and summed in bfloat16 or wider, within the bound.
No kernel may reach another device: no remote copies, remote signals or barrier semaphores. Data moves between devices by JAX's collectives and lax.ppermute only.
A program may use at most 128 MiB of HBM per device.

```python
import math
import jax
import jax.numpy as jnp
from jax import lax

WIDTH = 512
GROUPS = 8
CAP = 2048
TOKENS = 65536
N_SEQ = 32


def fast_weight(key, salt):
    base_key, row_key = jax.random.split(jax.random.fold_in(key, salt))
    base = jnp.clip(jax.random.normal(base_key, (GROUPS, WIDTH, WIDTH), jnp.float32), -4.0, 4.0)
    row_scale = jnp.exp(jax.random.uniform(row_key, (GROUPS, WIDTH, 1), jnp.float32, math.log(0.5), math.log(5.0)))
    return base * row_scale / math.sqrt(WIDTH)


def draw_w_first(key, part):
    return fast_weight(key, 11)


def draw_w_third(key, part):
    return fast_weight(key, 13)


def draw_w_second(key, part):
    return fast_weight(key, 17)


def draw_group_scales(key, part):
    ramp = jnp.arange(GROUPS, dtype=jnp.float32) / max(GROUPS - 1, 1)
    noise = jax.random.uniform(jax.random.fold_in(key, 23), (GROUPS,), jnp.float32, 0.85, 1.15)
    return 0.5 * jnp.exp(ramp * math.log(3.0)) * noise


def draw_live_counts(key, part):
    base_key, order_key, heavy_key = jax.random.split(jax.random.fold_in(key, 29), 3)
    light = jax.random.randint(base_key, (N_SEQ,), CAP // 8, CAP // 2 + 1)
    heavy = jax.random.randint(heavy_key, (N_SEQ,), CAP // 2, CAP + 1)
    order = jax.random.permutation(order_key, N_SEQ)
    counts = jnp.where(order < 3, heavy, light)
    return jnp.where(order == 0, CAP, counts).astype(jnp.int32)


def levels(own_key, extent, pieces, low, top_value):
    level, own = 1.0, jax.random.fold_in(own_key, 6)
    for dim, parts in pieces:
        heights = jnp.exp(jax.random.uniform(jax.random.fold_in(own, dim), (parts,), jnp.float32, low / len(pieces), top_value / len(pieces)))
        level = level * jnp.repeat(heights, extent[dim] // parts).reshape([-1 if axis == dim else 1 for axis in range(len(extent))])
    return level


def normal_values(own_key, dims, spread, bound, shards=(), kind=jnp.bfloat16):
    entries = spread * jax.random.normal(own_key, dims, jnp.float32)
    if shards:
        entries = entries * levels(own_key, dims, shards, -0.22, 0.18)
    return jnp.clip(entries, -bound, bound).astype(kind)


def setup_inputs(seed: int = 0) -> dict:
    arg_keys = jax.random.split(jax.random.key(seed), 10)
    return {
        "queries": normal_values(arg_keys[0], (TOKENS, GROUPS, WIDTH), 1.0, 6.0, ((0, 32), (1, 4))),
        "key_rows": normal_values(arg_keys[1], (TOKENS, GROUPS, WIDTH), 1.0, 6.0, ((0, 32), (1, 4))),
        "value_rows": normal_values(arg_keys[2], (TOKENS, GROUPS, WIDTH), 1.0, 6.0, ((0, 32), (1, 4))),
        "step_rates": jnp.clip(jnp.exp(math.log(4.0) - 2.7725887 * jax.random.uniform(arg_keys[3], (GROUPS, TOKENS), jnp.float32) ** levels(arg_keys[3], (GROUPS, TOKENS), ((0, 4), (1, 32)), -0.2, 0.2)), 0.25, 4.0).astype(jnp.bfloat16),
        "live_counts": draw_live_counts(jax.random.fold_in(arg_keys[9], 71), 0),
        "group_scales": draw_group_scales(jax.random.fold_in(arg_keys[9], 71), 0),
        "w_first": draw_w_first(jax.random.fold_in(arg_keys[9], 71), 0),
        "w_third": draw_w_third(jax.random.fold_in(arg_keys[9], 71), 0),
        "w_second": draw_w_second(jax.random.fold_in(arg_keys[9], 71), 0),
    }


EPS = 1e-06

def row_normalize(start_w, update):
    norm_old = jnp.sqrt(lax.optimization_barrier(jnp.mean(start_w * start_w, axis=-1, keepdims=True)) + EPS)
    norm_new = jnp.sqrt(lax.optimization_barrier(jnp.mean(update * update, axis=-1, keepdims=True)) + EPS)
    return update * (norm_old / norm_new)

def reference(queries, key_rows, value_rows, step_rates, live_counts, group_scales, w_first, w_third, w_second):
    total = queries.shape[0]
    position = jnp.arange(total, dtype=jnp.int32)
    owner_count = live_counts[position // CAP]
    live = position % CAP < owner_count
    live_f = live.astype(jnp.float32)
    live_b = live.astype(jnp.bfloat16)[:, None]
    root_total = math.sqrt(total)
    outputs = []
    for group in range(GROUPS):
        k_part = key_rows[:, group]
        v_part = value_rows[:, group]
        q_part = queries[:, group]
        eta = step_rates[group].astype(jnp.float32) * live_f / root_total
        b_one = w_first[group].astype(jnp.bfloat16)
        b_three = w_third[group].astype(jnp.bfloat16)
        b_two = w_second[group].astype(jnp.bfloat16)
        h_one = jnp.dot(k_part, b_one, preferred_element_type=jnp.float32)
        h_three = jnp.dot(k_part, b_three, preferred_element_type=jnp.float32)
        gate = jax.nn.silu(h_one)
        act = (gate * h_three).astype(jnp.bfloat16)
        err = (eta[:, None] * v_part.astype(jnp.float32)).astype(jnp.bfloat16)
        back = jnp.dot(err, b_two.T, preferred_element_type=jnp.float32)
        sig = jax.nn.sigmoid(h_one)
        d_one = (back * h_three * (sig * (1.0 + h_one * (1.0 - sig)))).astype(jnp.bfloat16)
        d_three = (back * gate).astype(jnp.bfloat16)
        p_one = jnp.dot(k_part.T, d_one, preferred_element_type=jnp.float32)
        p_three = jnp.dot(k_part.T, d_three, preferred_element_type=jnp.float32)
        p_two = jnp.dot(act.T, err, preferred_element_type=jnp.float32)
        c_one = row_normalize(w_first[group], w_first[group] + p_one).astype(jnp.bfloat16)
        c_three = row_normalize(w_third[group], w_third[group] + p_three).astype(jnp.bfloat16)
        c_two = row_normalize(w_second[group], w_second[group] + p_two).astype(jnp.bfloat16)
        q_one = jnp.dot(q_part, c_one, preferred_element_type=jnp.float32)
        q_three = jnp.dot(q_part, c_three, preferred_element_type=jnp.float32)
        a_query = (jax.nn.silu(q_one) * q_three).astype(jnp.bfloat16)
        o_part = jnp.dot(a_query, c_two, preferred_element_type=jnp.float32).astype(jnp.bfloat16) * live_b
        outputs.append(o_part.astype(jnp.float32) * group_scales[group])
    total_sq = jnp.zeros((total,), jnp.float32)
    for group in range(GROUPS):
        total_sq = total_sq + lax.optimization_barrier(jnp.sum(outputs[group] * outputs[group], axis=-1))
    factor = lax.rsqrt(total_sq / (GROUPS * WIDTH) + EPS)[:, None]
    return jnp.stack([(wide * factor).astype(jnp.bfloat16) for wide in outputs], axis=1)
```

```python
import jax
import jax.numpy as jnp
from jax import lax
from jax.sharding import PartitionSpec as P

EPS = 1e-06


def row_normalize(start_w, update):
    norm_old = jnp.sqrt(jnp.mean(start_w * start_w, axis=-1, keepdims=True) + EPS)
    norm_new = jnp.sqrt(jnp.mean(update * update, axis=-1, keepdims=True) + EPS)
    return update * (norm_old / norm_new)


def group_terms(k_part, v_part, eta_col, b_one, b_three, b_two):
    h_one = jnp.dot(k_part, b_one, preferred_element_type=jnp.float32)
    h_three = jnp.dot(k_part, b_three, preferred_element_type=jnp.float32)
    gate = jax.nn.silu(h_one)
    act = (gate * h_three).astype(jnp.bfloat16)
    err = (eta_col[:, None] * v_part.astype(jnp.float32)).astype(jnp.bfloat16)
    back = jnp.dot(err, b_two.T, preferred_element_type=jnp.float32)
    sig = jax.nn.sigmoid(h_one)
    d_one = (back * h_three * (sig * (1.0 + h_one * (1.0 - sig)))).astype(jnp.bfloat16)
    d_three = (back * gate).astype(jnp.bfloat16)
    p_one = jnp.dot(k_part.T, d_one, preferred_element_type=jnp.float32)
    p_three = jnp.dot(k_part.T, d_three, preferred_element_type=jnp.float32)
    p_two = jnp.dot(act.T, err, preferred_element_type=jnp.float32)
    return (p_one, p_three, p_two)


def shard_terms(k_rows, v_rows, eta_rows, halves):
    b_one, b_three, b_two = halves
    firsts, thirds, seconds = ([], [], [])
    for group in range(k_rows.shape[1]):
        p_one, p_three, p_two = group_terms(
            k_rows[:, group],
            v_rows[:, group],
            eta_rows[:, group],
            b_one[group],
            b_three[group],
            b_two[group],
        )
        firsts.append(p_one)
        thirds.append(p_three)
        seconds.append(p_two)
    return (jnp.stack(firsts), jnp.stack(thirds), jnp.stack(seconds))


def apply_rows(q_rows, live_mask, fresh):
    c_one, c_three, c_two = fresh
    live_b = live_mask.astype(jnp.bfloat16)[:, None]
    pieces = []
    for group in range(q_rows.shape[1]):
        q_part = q_rows[:, group]
        q_one = jnp.dot(q_part, c_one[group], preferred_element_type=jnp.float32)
        q_three = jnp.dot(q_part, c_three[group], preferred_element_type=jnp.float32)
        a_query = (jax.nn.silu(q_one) * q_three).astype(jnp.bfloat16)
        o_part = jnp.dot(a_query, c_two[group], preferred_element_type=jnp.float32).astype(
            jnp.bfloat16
        )
        pieces.append(o_part * live_b)
    return jnp.stack(pieces, axis=1)


def gather_rows(chunk):
    seq_size = lax.axis_size("seq")
    wide = jnp.broadcast_to(chunk[None], (seq_size,) + chunk.shape)
    blocks = lax.all_to_all(wide, "seq", 0, 0, tiled=True)
    mats, rows, width = chunk.shape
    return blocks.transpose(1, 0, 2, 3).reshape(mats, seq_size * rows, width)


def scatter_sum(terms):
    seq_size = lax.axis_size("seq")
    mats, rows, width = terms.shape
    blocks = terms.reshape(mats, seq_size, rows // seq_size, width).transpose(1, 0, 2, 3)
    blocks = lax.all_to_all(blocks.astype(jnp.bfloat16), "seq", 0, 0, tiled=True)
    return jnp.sum(blocks.astype(jnp.float32), axis=0)


def shards(
    queries, key_rows, value_rows, step_rates, live_counts, group_scales, w_first, w_third, w_second
):
    cap_rows, groups, feat_width = queries.shape
    seq_size = lax.axis_size("seq")
    root_total = jnp.sqrt(jnp.float32(cap_rows * seq_size))
    own_index = lax.axis_index("seq")
    own_count = live_counts[own_index]
    position = jnp.arange(cap_rows, dtype=jnp.int32)
    live_mask = position < own_count
    own_rows = jnp.concatenate((w_first, w_third, w_second), axis=0)
    halves = gather_rows(own_rows.astype(jnp.bfloat16))
    eta_rows = (
        step_rates.T.astype(jnp.float32) * live_mask.astype(jnp.float32)[:, None] / root_total
    )
    sums = shard_terms(
        key_rows, value_rows, eta_rows, (halves[:groups], halves[groups : 2 * groups], halves[2 * groups :])
    )
    summed = scatter_sum(jnp.concatenate(sums, axis=0))
    fresh_rows = row_normalize(own_rows, own_rows + summed).astype(jnp.bfloat16)
    fresh = gather_rows(fresh_rows)
    fresh = (fresh[:groups], fresh[groups : 2 * groups], fresh[2 * groups :])
    fast = apply_rows(queries, live_mask, fresh)
    wide = fast.astype(jnp.float32) * group_scales[None, :, None]
    partial_sq = jnp.sum(wide * wide, axis=(1, 2))
    total_sq = lax.psum(partial_sq, "heads")
    denom = groups * feat_width * lax.axis_size("heads")
    factor = lax.rsqrt(total_sq / denom + EPS)[:, None, None]
    return (wide * factor).astype(jnp.bfloat16)


def solution(mesh):
    in_specs = (
        P("seq", "heads", None),
        P("seq", "heads", None),
        P("seq", "heads", None),
        P("heads", "seq"),
        P(),
        P("heads"),
        P("heads", "seq", None),
        P("heads", "seq", None),
        P("heads", "seq", None),
    )
    out_specs = P("seq", "heads", None)
    return jax.shard_map(shards, mesh=mesh, in_specs=in_specs, out_specs=out_specs, check_vma=False)
```

```python
import functools
import jax
import jax.numpy as jnp
from jax import lax
from jax.experimental import pallas as pl
from jax.experimental.pallas import tpu as pltpu
from jax.sharding import PartitionSpec as P

EPS = 1e-06
VMEM_BYTES = 56 * 1024 * 1024
TERM_ROWS = 512
APPLY_ROWS = 512


def params():
    return pltpu.CompilerParams(vmem_limit_bytes=VMEM_BYTES)


def dot(a, b, dims):
    return lax.dot_general(a, b, (dims, ((), ())), preferred_element_type=jnp.float32)


def spread_kernel(w_first, w_third, w_second, wide):
    for mat, ref in enumerate((w_first, w_third, w_second)):
        part = ref[...].astype(jnp.bfloat16)
        for peer in range(wide.shape[0]):
            wide[peer, :, mat] = part


def spread(weights, peers):
    groups, rows, width = weights[0].shape
    return pl.pallas_call(
        spread_kernel,
        out_shape=jax.ShapeDtypeStruct((peers, groups, 3, rows, width), jnp.bfloat16),
        compiler_params=params(),
        name="spread",
    )(*weights)


def renew_kernel(blocks, w_first, w_third, w_second, wide):
    peers, groups = blocks.shape[:2]
    for mat, ref in enumerate((w_first, w_third, w_second)):
        for group in range(groups):
            term = jnp.sum(blocks[:, group, mat].astype(jnp.float32), axis=0)
            start = ref[group]
            update = start + term
            norm_old = jnp.mean(start * start, axis=-1, keepdims=True) + EPS
            norm_new = jnp.mean(update * update, axis=-1, keepdims=True) + EPS
            fresh = (update * (jnp.sqrt(norm_old) / jnp.sqrt(norm_new))).astype(jnp.bfloat16)
            for peer in range(peers):
                wide[peer, group, mat] = fresh


def renew(blocks, weights):
    return pl.pallas_call(
        renew_kernel,
        out_shape=jax.ShapeDtypeStruct(blocks.shape, jnp.bfloat16),
        compiler_params=params(),
        name="renew",
    )(blocks, *weights)


def terms_kernel(steps, k_ref, e_ref, b_ref, out, acc_in, acc_out):
    step = pl.program_id(1)
    width = k_ref.shape[1]
    k_part, err = k_ref[...], e_ref[...]
    b_one, b_three, b_two = (b_ref[:, 0, mat].reshape(width, width) for mat in range(3))
    h_one = dot(k_part, b_one, ((1,), (0,)))
    h_three = dot(k_part, b_three, ((1,), (0,)))
    back = dot(err, b_two, ((1,), (1,)))
    sig = jax.nn.sigmoid(h_one)
    gate = h_one * sig
    act = (gate * h_three).astype(jnp.bfloat16)
    d_one = (back * h_three * (sig * (1.0 + h_one * (1.0 - sig)))).astype(jnp.bfloat16)
    d_three = (back * gate).astype(jnp.bfloat16)
    p_in = dot(k_part, jnp.concatenate((d_one, d_three), axis=1), ((0,), (0,)))
    p_out = dot(act, err, ((0,), (0,)))

    @pl.when(step == 0)
    def _():
        acc_in[...] = p_in
        acc_out[...] = p_out

    @pl.when(step > 0)
    def _():
        acc_in[...] += p_in
        acc_out[...] += p_out

    @pl.when(step == steps - 1)
    def _():
        block = out.shape[:1] + out.shape[3:]
        out[:, 0, 0] = acc_in[:, :width].astype(jnp.bfloat16).reshape(block)
        out[:, 0, 1] = acc_in[:, width:].astype(jnp.bfloat16).reshape(block)
        out[:, 0, 2] = acc_out[...].astype(jnp.bfloat16).reshape(block)


def terms(k_flat, e_flat, halves):
    cap_rows = k_flat.shape[0]
    peers, groups, mats, rows, width = halves.shape
    steps = cap_rows // TERM_ROWS
    tokens = pl.BlockSpec((TERM_ROWS, width), lambda g, t: (t, g))
    weights = pl.BlockSpec((peers, 1, mats, rows, width), lambda g, t: (0, g, 0, 0, 0))
    return pl.pallas_call(
        functools.partial(terms_kernel, steps),
        grid=(groups, steps),
        in_specs=[tokens, tokens, weights],
        out_specs=weights,
        out_shape=jax.ShapeDtypeStruct(halves.shape, jnp.bfloat16),
        scratch_shapes=[
            pltpu.VMEM((width, 2 * width), jnp.float32),
            pltpu.VMEM((width, width), jnp.float32),
        ],
        compiler_params=params(),
        name="terms",
    )(k_flat, e_flat, halves)


def apply_kernel(q_ref, c_ref, live_ref, scale_ref, o_ref, ssq_ref):
    groups = c_ref.shape[1]
    width = q_ref.shape[1] // groups
    tokens = q_ref.shape[0]
    first = pl.program_id(0) * tokens
    live = first + lax.broadcasted_iota(jnp.int32, (tokens, width), 0) < live_ref[0]
    squares = jnp.zeros((tokens, 128), jnp.float32)
    for group in range(groups):
        q_part = q_ref[:, group * width : (group + 1) * width]
        c_one, c_three, c_two = (c_ref[:, group, mat].reshape(width, width) for mat in range(3))
        q_one = dot(q_part, c_one, ((1,), (0,)))
        q_three = dot(q_part, c_three, ((1,), (0,)))
        a_query = (q_one * jax.nn.sigmoid(q_one) * q_three).astype(jnp.bfloat16)
        o_part = dot(a_query, c_two, ((1,), (0,)))
        o_part = jnp.where(live, o_part, 0.0).astype(jnp.bfloat16)
        o_ref[:, group * width : (group + 1) * width] = o_part
        scaled = o_part.astype(jnp.float32) * scale_ref[group]
        scaled = scaled * scaled
        for col in range(width // 128):
            squares = squares + scaled[:, col * 128 : (col + 1) * 128]
    ssq_ref[...] = jnp.sum(squares.T, axis=0, keepdims=True)


def apply(q_flat, fresh, own_count, scales):
    cap_rows, both = q_flat.shape
    steps = cap_rows // APPLY_ROWS
    tokens = pl.BlockSpec((APPLY_ROWS, both), lambda t: (t, 0))
    return pl.pallas_call(
        apply_kernel,
        grid=(steps,),
        in_specs=[
            tokens,
            pl.BlockSpec(fresh.shape, lambda t: (0, 0, 0, 0, 0)),
            pl.BlockSpec(memory_space=pltpu.SMEM),
            pl.BlockSpec(memory_space=pltpu.SMEM),
        ],
        out_specs=[tokens, pl.BlockSpec((1, APPLY_ROWS), lambda t: (0, t))],
        out_shape=[
            jax.ShapeDtypeStruct(q_flat.shape, jnp.bfloat16),
            jax.ShapeDtypeStruct((1, cap_rows), jnp.float32),
        ],
        compiler_params=params(),
        name="apply",
    )(q_flat, fresh, own_count, scales)


def exchange(blocks):
    return lax.all_to_all(blocks, "seq", 0, 0, tiled=True)


def shards(
    queries, key_rows, value_rows, step_rates, live_counts, group_scales, w_first, w_third, w_second
):
    cap_rows, groups, feat_width = queries.shape
    seq_size = lax.axis_size("seq")
    root_total = jnp.sqrt(jnp.float32(cap_rows * seq_size))
    own_count = live_counts[lax.axis_index("seq")]
    live_mask = jnp.arange(cap_rows, dtype=jnp.int32) < own_count
    weights = (w_first, w_third, w_second)
    halves = exchange(spread(weights, seq_size))
    eta = step_rates.T.astype(jnp.float32) * live_mask.astype(jnp.float32)[:, None] / root_total
    err = (eta[:, :, None] * value_rows.astype(jnp.float32)).astype(jnp.bfloat16)
    flat = (cap_rows, groups * feat_width)
    sums = exchange(terms(key_rows.reshape(flat), err.reshape(flat), halves))
    fresh = exchange(renew(sums, weights))
    fast, partial_sq = apply(queries.reshape(flat), fresh, own_count[None], group_scales)
    total_sq = lax.psum(partial_sq[0], "heads")
    denom = groups * feat_width * lax.axis_size("heads")
    factor = lax.rsqrt(total_sq / denom + EPS)[:, None, None]
    wide = fast.reshape(queries.shape).astype(jnp.float32) * group_scales[None, :, None]
    return (wide * factor).astype(jnp.bfloat16)


def solution(mesh):
    in_specs = (
        P("seq", "heads", None),
        P("seq", "heads", None),
        P("seq", "heads", None),
        P("heads", "seq"),
        P(),
        P("heads"),
        P("heads", "seq", None),
        P("heads", "seq", None),
        P("heads", "seq", None),
    )
    out_specs = P("seq", "heads", None)
    return jax.shard_map(shards, mesh=mesh, in_specs=in_specs, out_specs=out_specs, check_vma=False)
```

```python
import functools
import jax
import jax.numpy as jnp
from jax import lax
from jax.experimental import pallas as pl
from jax.experimental.pallas import tpu as pltpu
from jax.sharding import PartitionSpec as P

EPS = 1e-06
TERM_ROWS = 2048
APPLY_ROWS = 512
FINISH_ROWS = 512


def params(mebibytes):
    return pltpu.CompilerParams(vmem_limit_bytes=mebibytes * 1024 * 1024)


def dot(a, b, dims):
    return lax.dot_general(a, b, (dims, ((), ())), preferred_element_type=jnp.float32)


def spread_kernel(w_first, w_third, w_second, wide):
    for mat, ref in enumerate((w_first, w_third, w_second)):
        part = ref[...].astype(jnp.bfloat16)
        for peer in range(wide.shape[0]):
            wide[peer, :, mat] = part


def spread(weights, peers):
    groups, rows, width = weights[0].shape
    return pl.pallas_call(
        spread_kernel,
        out_shape=jax.ShapeDtypeStruct((peers, groups, 3, rows, width), jnp.bfloat16),
        compiler_params=params(16),
        name="spread",
    )(*weights)


def renew_kernel(blocks, w_first, w_third, w_second, wide):
    peers, groups = blocks.shape[:2]
    for mat, ref in enumerate((w_first, w_third, w_second)):
        for group in range(groups):
            term = jnp.sum(blocks[:, group, mat].astype(jnp.float32), axis=0)
            start = ref[group]
            update = start + term
            norm_old = jnp.mean(start * start, axis=-1, keepdims=True) + EPS
            norm_new = jnp.mean(update * update, axis=-1, keepdims=True) + EPS
            fresh = (update * (jnp.sqrt(norm_old) / jnp.sqrt(norm_new))).astype(jnp.bfloat16)
            for peer in range(peers):
                wide[peer, group, mat] = fresh


def renew(blocks, weights):
    return pl.pallas_call(
        renew_kernel,
        out_shape=jax.ShapeDtypeStruct(blocks.shape, jnp.bfloat16),
        compiler_params=params(24),
        name="renew",
    )(blocks, *weights)


def terms_kernel(steps, k_ref, e_ref, b_ref, out, acc_in, acc_out):
    group, step = pl.program_id(0), pl.program_id(1)
    width = k_ref.shape[1]
    k_part, err = k_ref[...], e_ref[...]
    b_one, b_three, b_two = (b_ref[:, group, mat].reshape(width, width) for mat in range(3))
    h_one = dot(k_part, b_one, ((1,), (0,)))
    h_three = dot(k_part, b_three, ((1,), (0,)))
    back = dot(err, b_two, ((1,), (1,)))
    sig = jax.nn.sigmoid(h_one)
    gate = h_one * sig
    act = (gate * h_three).astype(jnp.bfloat16)
    d_one = (back * h_three * (sig * (1.0 + h_one * (1.0 - sig)))).astype(jnp.bfloat16)
    d_three = (back * gate).astype(jnp.bfloat16)
    p_in = dot(k_part, jnp.concatenate((d_one, d_three), axis=1), ((0,), (0,)))
    p_out = dot(act, err, ((0,), (0,)))

    @pl.when(step == 0)
    def _():
        acc_in[...] = p_in
        acc_out[...] = p_out

    @pl.when(step > 0)
    def _():
        acc_in[...] += p_in
        acc_out[...] += p_out

    @pl.when(step == steps - 1)
    def _():
        block = out.shape[:1] + out.shape[3:]
        out[:, 0, 0] = acc_in[:, :width].astype(jnp.bfloat16).reshape(block)
        out[:, 0, 1] = acc_in[:, width:].astype(jnp.bfloat16).reshape(block)
        out[:, 0, 2] = acc_out[...].astype(jnp.bfloat16).reshape(block)


def terms(k_flat, e_flat, halves):
    cap_rows = k_flat.shape[0]
    peers, groups, mats, rows, width = halves.shape
    steps = cap_rows // TERM_ROWS
    tokens = pl.BlockSpec((TERM_ROWS, width), lambda g, t: (t, g))
    weights = pl.BlockSpec((peers, 1, mats, rows, width), lambda g, t: (0, g, 0, 0, 0))
    return pl.pallas_call(
        functools.partial(terms_kernel, steps),
        grid=(groups, steps),
        in_specs=[tokens, tokens, pl.BlockSpec(memory_space=pltpu.VMEM)],
        out_specs=weights,
        out_shape=jax.ShapeDtypeStruct(halves.shape, jnp.bfloat16),
        scratch_shapes=[
            pltpu.VMEM((width, 2 * width), jnp.float32),
            pltpu.VMEM((width, width), jnp.float32),
        ],
        compiler_params=params(40),
        name="terms",
    )(k_flat, e_flat, halves)


def apply_kernel(q_ref, c_ref, live_ref, scale_ref, o_ref, ssq_ref):
    groups = c_ref.shape[1]
    width = q_ref.shape[1] // groups
    tokens = q_ref.shape[0]
    first = pl.program_id(0) * tokens
    live = first + lax.broadcasted_iota(jnp.int32, (tokens, width), 0) < live_ref[0]
    squares = jnp.zeros((tokens, 128), jnp.float32)
    for group in range(groups):
        q_part = q_ref[:, group * width : (group + 1) * width]
        c_one, c_three, c_two = (c_ref[:, group, mat].reshape(width, width) for mat in range(3))
        q_one = dot(q_part, c_one, ((1,), (0,)))
        q_three = dot(q_part, c_three, ((1,), (0,)))
        a_query = (q_one * jax.nn.sigmoid(q_one) * q_three).astype(jnp.bfloat16)
        o_part = dot(a_query, c_two, ((1,), (0,)))
        o_part = jnp.where(live, o_part, 0.0).astype(jnp.bfloat16)
        o_ref[:, group * width : (group + 1) * width] = o_part
        scaled = o_part.astype(jnp.float32) * scale_ref[group]
        scaled = scaled * scaled
        for col in range(width // 128):
            squares = squares + scaled[:, col * 128 : (col + 1) * 128]
    ssq_ref[...] = jnp.sum(squares.T, axis=0, keepdims=True)


def apply(q_flat, fresh, own_count, scales):
    cap_rows, both = q_flat.shape
    steps = cap_rows // APPLY_ROWS
    tokens = pl.BlockSpec((APPLY_ROWS, both), lambda t: (t, 0))
    return pl.pallas_call(
        apply_kernel,
        grid=(steps,),
        in_specs=[
            tokens,
            pl.BlockSpec(memory_space=pltpu.VMEM),
            pl.BlockSpec(memory_space=pltpu.SMEM),
            pl.BlockSpec(memory_space=pltpu.SMEM),
        ],
        out_specs=[tokens, pl.BlockSpec((1, APPLY_ROWS), lambda t: (0, t))],
        out_shape=[
            jax.ShapeDtypeStruct(q_flat.shape, jnp.bfloat16),
            jax.ShapeDtypeStruct((1, cap_rows), jnp.float32),
        ],
        compiler_params=params(24),
        name="apply",
    )(q_flat, fresh, own_count, scales)


def finish_kernel(o_ref, ssq_ref, scale_ref, out):
    tokens, both = o_ref.shape
    groups = scale_ref.shape[0]
    width = both // groups
    lanes = 128
    tiles = width // lanes
    side = 256
    span = side // (groups * tiles)
    factor = lax.rsqrt(ssq_ref[...] * scale_ref[groups - 1, 1] + EPS)
    factor = jnp.broadcast_to(factor, (lanes, tokens)).T
    columns = []
    for start in range(0, tokens, span):
        rows = slice(start, start + span)
        pieces = []
        for group in range(groups):
            for tile in range(tiles):
                col = group * width + tile * lanes
                part = o_ref[rows, col : col + lanes].astype(jnp.float32) * scale_ref[group, 0]
                pieces.append(part * factor[rows])
        columns.append(jnp.concatenate(pieces, axis=0).astype(jnp.bfloat16))
    row = lax.broadcasted_iota(jnp.int32, (side, side), 0)
    col = lax.broadcasted_iota(jnp.int32, (side, side), 1)
    token, tile, group = row // (groups * tiles), row % (groups * tiles) // groups, row % groups
    order = jnp.where(col == (group * tiles + tile) * span + token, 1.0, 0.0).astype(jnp.bfloat16)
    mixed = dot(order, jnp.concatenate(columns, axis=1), ((1,), (0,))).astype(jnp.bfloat16)
    for index in range(len(columns)):
        out[index * side : (index + 1) * side] = mixed[:, index * lanes : (index + 1) * lanes]


def finish(fast, total_sq, scales):
    cap_rows, both = fast.shape
    lanes = 128
    rows = FINISH_ROWS * both // lanes
    return pl.pallas_call(
        finish_kernel,
        grid=(cap_rows // FINISH_ROWS,),
        in_specs=[
            pl.BlockSpec((FINISH_ROWS, both), lambda t: (t, 0)),
            pl.BlockSpec((1, FINISH_ROWS), lambda t: (0, t)),
            pl.BlockSpec(memory_space=pltpu.SMEM),
        ],
        out_specs=pl.BlockSpec((rows, lanes), lambda t: (t, 0)),
        out_shape=jax.ShapeDtypeStruct((cap_rows * both // lanes, lanes), jnp.bfloat16),
        compiler_params=params(16),
        name="finish",
    )(fast, total_sq, scales)


def exchange(blocks):
    return lax.all_to_all(blocks, "seq", 0, 0, tiled=True)


def shards(
    queries, key_rows, value_rows, step_rates, live_counts, group_scales, w_first, w_third, w_second
):
    cap_rows, groups, feat_width = queries.shape
    seq_size = lax.axis_size("seq")
    root_total = jnp.sqrt(jnp.float32(cap_rows * seq_size))
    own_count = live_counts[lax.axis_index("seq")]
    live_mask = jnp.arange(cap_rows, dtype=jnp.int32) < own_count
    weights = (w_first, w_third, w_second)
    halves = exchange(spread(weights, seq_size))
    eta = step_rates.T.astype(jnp.float32) * live_mask.astype(jnp.float32)[:, None] / root_total
    err = (eta[:, :, None] * value_rows.astype(jnp.float32)).astype(jnp.bfloat16)
    flat = (cap_rows, groups * feat_width)
    sums = exchange(terms(key_rows.reshape(flat), err.reshape(flat), halves))
    fresh = exchange(renew(sums, weights))
    fast, partial_sq = apply(queries.reshape(flat), fresh, own_count[None], group_scales)
    total_sq = lax.psum(partial_sq, "heads")
    share = jnp.full_like(group_scales, 1.0 / (groups * feat_width * lax.axis_size("heads")))
    ordered = finish(fast, total_sq, jnp.stack((group_scales, share), axis=1))
    ordered = ordered.reshape(cap_rows, feat_width // 128, groups, 128).transpose(0, 2, 1, 3)
    return ordered.reshape(queries.shape)


def solution(mesh):
    in_specs = (
        P("seq", "heads", None),
        P("seq", "heads", None),
        P("seq", "heads", None),
        P("heads", "seq"),
        P(),
        P("heads"),
        P("heads", "seq", None),
        P("heads", "seq", None),
        P("heads", "seq", None),
    )
    out_specs = P("seq", "heads", None)
    return jax.shard_map(shards, mesh=mesh, in_specs=in_specs, out_specs=out_specs, check_vma=False)
```

```python
import functools
import jax
import jax.numpy as jnp
from jax import lax
from jax.experimental import pallas as pl
from jax.experimental.pallas import tpu as pltpu
from jax.sharding import PartitionSpec as P

EPS = 1e-06
TERM_ROWS = 512
SPREAD_MIB = 60
TERMS_MIB = 46
APPLY_MIB = 50
FINISH_MIB = 58
APPLY_ROWS = 512
FINISH_ROWS = 512


def params(mebibytes):
    return pltpu.CompilerParams(vmem_limit_bytes=mebibytes * 1024 * 1024)


def dot(a, b, dims):
    return lax.dot_general(a, b, (dims, ((), ())), preferred_element_type=jnp.float32)


def send_all(chunk, wide, sems):
    copies = [pltpu.make_async_copy(chunk, wide.at[peer], sems.at[peer]) for peer in range(wide.shape[0])]
    for copy in copies:
        copy.start()
    for copy in copies:
        copy.wait()


def spread_kernel(w_first, w_third, w_second, wide, chunk, sems):
    for mat, ref in enumerate((w_first, w_third, w_second)):
        chunk[:, mat] = ref[...].astype(jnp.bfloat16)
    send_all(chunk, wide, sems)


def spread(weights, peers):
    groups, rows, width = weights[0].shape
    return pl.pallas_call(
        spread_kernel,
        out_specs=pl.BlockSpec(memory_space=pl.ANY),
        out_shape=jax.ShapeDtypeStruct((peers, groups, 3, rows, width), jnp.bfloat16),
        scratch_shapes=[
            pltpu.VMEM((groups, 3, rows, width), jnp.bfloat16),
            pltpu.SemaphoreType.DMA((peers,)),
        ],
        compiler_params=params(SPREAD_MIB),
        name="spread",
    )(*weights)


def renew_kernel(blocks, w_first, w_third, w_second, wide, chunk, sems):
    groups = blocks.shape[1]
    for mat, ref in enumerate((w_first, w_third, w_second)):
        for group in range(groups):
            term = jnp.sum(blocks[:, group, mat].astype(jnp.float32), axis=0)
            start = ref[group]
            update = start + term
            norm_old = jnp.mean(start * start, axis=-1, keepdims=True) + EPS
            norm_new = jnp.mean(update * update, axis=-1, keepdims=True) + EPS
            fresh = update * (jnp.sqrt(norm_old) / jnp.sqrt(norm_new))
            chunk[group, mat] = fresh.astype(jnp.bfloat16)
    send_all(chunk, wide, sems)


def renew(blocks, weights):
    return pl.pallas_call(
        renew_kernel,
        out_specs=pl.BlockSpec(memory_space=pl.ANY),
        out_shape=jax.ShapeDtypeStruct(blocks.shape, jnp.bfloat16),
        scratch_shapes=[
            pltpu.VMEM(blocks.shape[1:], jnp.bfloat16),
            pltpu.SemaphoreType.DMA(blocks.shape[:1]),
        ],
        compiler_params=params(24),
        name="renew",
    )(blocks, *weights)


def terms_kernel(k_hbm, e_hbm, b_ref, out, k_ref, e_ref, d_ref, a_ref, k_sems, e_sems):
    groups = b_ref.shape[1]
    cap_rows = k_hbm.shape[0]
    width = k_hbm.shape[1] // groups
    block = out.shape[:1] + out.shape[3:]
    copies = {}
    for group in range(groups):
        cols = pl.ds(group * width, width)
        for part in range(cap_rows // TERM_ROWS):
            rows = pl.ds(part * TERM_ROWS, TERM_ROWS)
            copies[group, part] = (
                pltpu.make_async_copy(k_hbm.at[rows, cols], k_ref.at[group, rows], k_sems.at[group, part]),
                pltpu.make_async_copy(e_hbm.at[rows, cols], e_ref.at[group, rows], e_sems.at[group, part]),
            )
            for copy in copies[group, part]:
                copy.start()
    for group in range(groups):
        b_one, b_three, b_two = (b_ref[:, group, mat].reshape(width, width) for mat in range(3))
        for part in range(cap_rows // TERM_ROWS):
            for copy in copies[group, part]:
                copy.wait()
            rows = slice(part * TERM_ROWS, (part + 1) * TERM_ROWS)
            k_part, err = k_ref[group, rows], e_ref[group, rows]
            h_one = dot(k_part, b_one, ((1,), (0,)))
            h_three = dot(k_part, b_three, ((1,), (0,)))
            back = dot(err, b_two, ((1,), (1,)))
            sig = 0.5 * jnp.tanh(0.5 * h_one) + 0.5
            gate = h_one * sig
            a_ref[rows] = (gate * h_three).astype(jnp.bfloat16)
            d_ref[rows, :width] = (back * h_three * (sig + gate * (1.0 - sig))).astype(jnp.bfloat16)
            d_ref[rows, width:] = (back * gate).astype(jnp.bfloat16)
        p_in = dot(k_ref[group], d_ref[...], ((0,), (0,)))
        out[:, group, 0] = p_in[:, :width].astype(jnp.bfloat16).reshape(block)
        out[:, group, 1] = p_in[:, width:].astype(jnp.bfloat16).reshape(block)
        p_out = dot(a_ref[...], e_ref[group], ((0,), (0,)))
        out[:, group, 2] = p_out.astype(jnp.bfloat16).reshape(block)


def terms(k_flat, e_flat, halves):
    cap_rows = k_flat.shape[0]
    groups, width = halves.shape[1], halves.shape[4]
    parts = cap_rows // TERM_ROWS
    return pl.pallas_call(
        terms_kernel,
        in_specs=[
            pl.BlockSpec(memory_space=pl.ANY),
            pl.BlockSpec(memory_space=pl.ANY),
            pl.BlockSpec(memory_space=pltpu.VMEM),
        ],
        out_specs=pl.BlockSpec(memory_space=pltpu.VMEM),
        out_shape=jax.ShapeDtypeStruct(halves.shape, jnp.bfloat16),
        scratch_shapes=[
            pltpu.VMEM((groups, cap_rows, width), jnp.bfloat16),
            pltpu.VMEM((groups, cap_rows, width), jnp.bfloat16),
            pltpu.VMEM((cap_rows, 2 * width), jnp.bfloat16),
            pltpu.VMEM((cap_rows, width), jnp.bfloat16),
            pltpu.SemaphoreType.DMA((groups, parts)),
            pltpu.SemaphoreType.DMA((groups, parts)),
        ],
        compiler_params=params(TERMS_MIB),
        name="terms",
    )(k_flat, e_flat, halves)


def apply_kernel(q_ref, c_ref, live_ref, scale_ref, o_ref, ssq_ref):
    groups = c_ref.shape[1]
    width = q_ref.shape[1] // groups
    tokens = q_ref.shape[0]
    first = pl.program_id(0) * tokens
    live = first + lax.broadcasted_iota(jnp.int32, (tokens, width), 0) < live_ref[0]
    squares = jnp.zeros((tokens, 128), jnp.float32)
    for group in range(groups):
        q_part = q_ref[:, group * width : (group + 1) * width]
        c_one, c_three, c_two = (c_ref[:, group, mat].reshape(width, width) for mat in range(3))
        q_one = dot(q_part, c_one, ((1,), (0,)))
        q_three = dot(q_part, c_three, ((1,), (0,)))
        a_query = (q_one * (0.5 * jnp.tanh(0.5 * q_one) + 0.5) * q_three).astype(jnp.bfloat16)
        o_part = dot(a_query, c_two, ((1,), (0,)))
        o_part = jnp.where(live, o_part, 0.0).astype(jnp.bfloat16)
        o_ref[:, group * width : (group + 1) * width] = o_part
        scaled = o_part.astype(jnp.float32) * scale_ref[group]
        scaled = scaled * scaled
        for col in range(width // 128):
            squares = squares + scaled[:, col * 128 : (col + 1) * 128]
    ssq_ref[...] = jnp.sum(squares.T, axis=0, keepdims=True)


def apply(q_flat, fresh, own_count, scales):
    cap_rows, both = q_flat.shape
    steps = cap_rows // APPLY_ROWS
    tokens = pl.BlockSpec((APPLY_ROWS, both), lambda t: (t, 0))
    return pl.pallas_call(
        apply_kernel,
        grid=(steps,),
        in_specs=[
            tokens,
            pl.BlockSpec(memory_space=pltpu.VMEM),
            pl.BlockSpec(memory_space=pltpu.SMEM),
            pl.BlockSpec(memory_space=pltpu.SMEM),
        ],
        out_specs=[tokens, pl.BlockSpec((1, APPLY_ROWS), lambda t: (0, t))],
        out_shape=[
            jax.ShapeDtypeStruct(q_flat.shape, jnp.bfloat16),
            jax.ShapeDtypeStruct((1, cap_rows), jnp.float32),
        ],
        compiler_params=params(APPLY_MIB),
        name="apply",
    )(q_flat, fresh, own_count, scales)


def finish_kernel(o_ref, ssq_ref, scale_ref, out):
    tokens, both = o_ref.shape
    groups = scale_ref.shape[0]
    width = both // groups
    lanes = 128
    tiles = width // lanes
    side = 256
    span = side // (groups * tiles)
    total_sq = jnp.sum(ssq_ref[...], axis=0, keepdims=True)
    factor = lax.rsqrt(total_sq * scale_ref[groups - 1, 1] + EPS)
    factor = jnp.broadcast_to(factor, (lanes, tokens)).T
    columns = []
    for start in range(0, tokens, span):
        rows = slice(start, start + span)
        pieces = []
        for group in range(groups):
            for tile in range(tiles):
                col = group * width + tile * lanes
                part = o_ref[rows, col : col + lanes].astype(jnp.float32) * scale_ref[group, 0]
                pieces.append(part * factor[rows])
        columns.append(jnp.concatenate(pieces, axis=0).astype(jnp.bfloat16))
    row = lax.broadcasted_iota(jnp.int32, (side, side), 0)
    col = lax.broadcasted_iota(jnp.int32, (side, side), 1)
    token, tile, group = row // (groups * tiles), row % (groups * tiles) // groups, row % groups
    order = jnp.where(col == (group * tiles + tile) * span + token, 1.0, 0.0).astype(jnp.bfloat16)
    mixed = dot(order, jnp.concatenate(columns, axis=1), ((1,), (0,))).astype(jnp.bfloat16)
    for index in range(len(columns)):
        out[index * side : (index + 1) * side] = mixed[:, index * lanes : (index + 1) * lanes]


def finish(fast, total_sq, scales):
    cap_rows, both = fast.shape
    lanes = 128
    rows = FINISH_ROWS * both // lanes
    return pl.pallas_call(
        finish_kernel,
        grid=(cap_rows // FINISH_ROWS,),
        in_specs=[
            pl.BlockSpec((FINISH_ROWS, both), lambda t: (t, 0)),
            pl.BlockSpec((total_sq.shape[0], FINISH_ROWS), lambda t: (0, t)),
            pl.BlockSpec(memory_space=pltpu.SMEM),
        ],
        out_specs=pl.BlockSpec((rows, lanes), lambda t: (t, 0)),
        out_shape=jax.ShapeDtypeStruct((cap_rows * both // lanes, lanes), jnp.bfloat16),
        compiler_params=params(FINISH_MIB),
        name="finish",
    )(fast, total_sq, scales)


def exchange(blocks):
    return lax.all_to_all(blocks, "seq", 0, 0, tiled=True)


def shards(
    queries, key_rows, value_rows, step_rates, live_counts, group_scales, w_first, w_third, w_second
):
    cap_rows, groups, feat_width = queries.shape
    seq_size = lax.axis_size("seq")
    root_total = jnp.sqrt(jnp.float32(cap_rows * seq_size))
    own_count = live_counts[lax.axis_index("seq")]
    live_mask = jnp.arange(cap_rows, dtype=jnp.int32) < own_count
    weights = (w_first, w_third, w_second)
    halves = exchange(spread(weights, seq_size))
    eta = step_rates.T.astype(jnp.float32) * live_mask.astype(jnp.float32)[:, None] / root_total
    err = (eta[:, :, None] * value_rows.astype(jnp.float32)).astype(jnp.bfloat16)
    flat = (cap_rows, groups * feat_width)
    sums = exchange(terms(key_rows.reshape(flat), err.reshape(flat), halves))
    fresh = exchange(renew(sums, weights))
    fast, partial_sq = apply(queries.reshape(flat), fresh, own_count[None], group_scales)
    total_sq = lax.all_gather(partial_sq, "heads", axis=0, tiled=True)
    share = jnp.full_like(group_scales, 1.0 / (groups * feat_width * lax.axis_size("heads")))
    ordered = finish(fast, total_sq, jnp.stack((group_scales, share), axis=1))
    ordered = ordered.reshape(cap_rows, feat_width // 128, groups, 128).transpose(0, 2, 1, 3)
    return ordered.reshape(queries.shape)


def solution(mesh):
    in_specs = (
        P("seq", "heads", None),
        P("seq", "heads", None),
        P("seq", "heads", None),
        P("heads", "seq"),
        P(),
        P("heads"),
        P("heads", "seq", None),
        P("heads", "seq", None),
        P("heads", "seq", None),
    )
    out_specs = P("seq", "heads", None)
    return jax.shard_map(shards, mesh=mesh, in_specs=in_specs, out_specs=out_specs, check_vma=False)
```

```python
import functools
import jax
import jax.numpy as jnp
from jax import lax
from jax.experimental import pallas as pl
from jax.experimental.pallas import tpu as pltpu
from jax.sharding import PartitionSpec as P

EPS = 1e-06
TERM_ROWS = 512
SPREAD_MIB = 60
TERMS_MIB = 46
APPLY_MIB = 50
FINISH_MIB = 58
APPLY_ROWS = 512
FINISH_ROWS = 1024


def params(mebibytes):
    return pltpu.CompilerParams(vmem_limit_bytes=mebibytes * 1024 * 1024)


def dot(a, b, dims):
    return lax.dot_general(a, b, (dims, ((), ())), preferred_element_type=jnp.float32)


def send_all(chunk, wide, sems):
    copies = [pltpu.make_async_copy(chunk, wide.at[peer], sems.at[peer]) for peer in range(wide.shape[0])]
    for copy in copies:
        copy.start()
    for copy in copies:
        copy.wait()


def spread_kernel(w_first, w_third, w_second, wide, chunk, sems):
    for mat, ref in enumerate((w_first, w_third, w_second)):
        chunk[:, mat] = ref[...].astype(jnp.bfloat16)
    send_all(chunk, wide, sems)


def spread(weights, peers):
    groups, rows, width = weights[0].shape
    return pl.pallas_call(
        spread_kernel,
        out_specs=pl.BlockSpec(memory_space=pl.ANY),
        out_shape=jax.ShapeDtypeStruct((peers, groups, 3, rows, width), jnp.bfloat16),
        scratch_shapes=[
            pltpu.VMEM((groups, 3, rows, width), jnp.bfloat16),
            pltpu.SemaphoreType.DMA((peers,)),
        ],
        compiler_params=params(SPREAD_MIB),
        name="spread",
    )(*weights)


def renew_kernel(blocks, w_first, w_third, w_second, wide, chunk, sems):
    groups = blocks.shape[1]
    for mat, ref in enumerate((w_first, w_third, w_second)):
        for group in range(groups):
            term = jnp.sum(blocks[:, group, mat].astype(jnp.float32), axis=0)
            start = ref[group]
            update = start + term
            norm_old = jnp.mean(start * start, axis=-1, keepdims=True) + EPS
            norm_new = jnp.mean(update * update, axis=-1, keepdims=True) + EPS
            fresh = update * (jnp.sqrt(norm_old) / jnp.sqrt(norm_new))
            chunk[group, mat] = fresh.astype(jnp.bfloat16)
    send_all(chunk, wide, sems)


def renew(blocks, weights):
    return pl.pallas_call(
        renew_kernel,
        out_specs=pl.BlockSpec(memory_space=pl.ANY),
        out_shape=jax.ShapeDtypeStruct(blocks.shape, jnp.bfloat16),
        scratch_shapes=[
            pltpu.VMEM(blocks.shape[1:], jnp.bfloat16),
            pltpu.SemaphoreType.DMA(blocks.shape[:1]),
        ],
        compiler_params=params(24),
        name="renew",
    )(blocks, *weights)


def arrivals(group, part, parts):
    if group == 0 and part == 0:
        return [0]
    if part == (1 if group == 0 else 0):
        return range(part, parts)
    return []


def terms_kernel(k_hbm, e_hbm, b_ref, out, k_ref, e_ref, d_ref, a_ref, k_sems, e_sems):
    groups = b_ref.shape[1]
    cap_rows = k_hbm.shape[0]
    width = k_hbm.shape[1] // groups
    block = out.shape[:1] + out.shape[3:]
    copies = {}
    for group in range(groups):
        cols = pl.ds(group * width, width)
        for part in range(cap_rows // TERM_ROWS):
            rows = pl.ds(part * TERM_ROWS, TERM_ROWS)
            copies[group, part] = (
                pltpu.make_async_copy(k_hbm.at[rows, cols], k_ref.at[group, rows], k_sems.at[group, part]),
                pltpu.make_async_copy(e_hbm.at[rows, cols], e_ref.at[group, rows], e_sems.at[group, part]),
            )
            for copy in copies[group, part]:
                copy.start()
    for group in range(groups):
        b_one, b_three, b_two = (b_ref[:, group, mat].reshape(width, width) for mat in range(3))
        for part in range(cap_rows // TERM_ROWS):
            for arrival in arrivals(group, part, cap_rows // TERM_ROWS):
                for copy in copies[group, arrival]:
                    copy.wait()
            rows = slice(part * TERM_ROWS, (part + 1) * TERM_ROWS)
            k_part, err = k_ref[group, rows], e_ref[group, rows]
            h_one = dot(k_part, b_one, ((1,), (0,)))
            h_three = dot(k_part, b_three, ((1,), (0,)))
            back = dot(err, b_two, ((1,), (1,)))
            half = 0.5 * h_one
            turn = jnp.tanh(half)
            gate = half * turn + half
            sig = 0.5 * turn + 0.5
            a_ref[rows] = (gate * h_three).astype(jnp.bfloat16)
            d_ref[rows, :width] = (back * h_three * (sig + gate * (1.0 - sig))).astype(jnp.bfloat16)
            d_ref[rows, width:] = (back * gate).astype(jnp.bfloat16)
        p_in = dot(k_ref[group], d_ref[...], ((0,), (0,)))
        out[:, group, 0] = p_in[:, :width].astype(jnp.bfloat16).reshape(block)
        out[:, group, 1] = p_in[:, width:].astype(jnp.bfloat16).reshape(block)
        p_out = dot(a_ref[...], e_ref[group], ((0,), (0,)))
        out[:, group, 2] = p_out.astype(jnp.bfloat16).reshape(block)


def terms(k_flat, e_flat, halves):
    cap_rows = k_flat.shape[0]
    groups, width = halves.shape[1], halves.shape[4]
    parts = cap_rows // TERM_ROWS
    return pl.pallas_call(
        terms_kernel,
        in_specs=[
            pl.BlockSpec(memory_space=pl.ANY),
            pl.BlockSpec(memory_space=pl.ANY),
            pl.BlockSpec(memory_space=pltpu.VMEM),
        ],
        out_specs=pl.BlockSpec(memory_space=pltpu.VMEM),
        out_shape=jax.ShapeDtypeStruct(halves.shape, jnp.bfloat16),
        scratch_shapes=[
            pltpu.VMEM((groups, cap_rows, width), jnp.bfloat16),
            pltpu.VMEM((groups, cap_rows, width), jnp.bfloat16),
            pltpu.VMEM((cap_rows, 2 * width), jnp.bfloat16),
            pltpu.VMEM((cap_rows, width), jnp.bfloat16),
            pltpu.SemaphoreType.DMA((groups, parts)),
            pltpu.SemaphoreType.DMA((groups, parts)),
        ],
        compiler_params=params(TERMS_MIB),
        name="terms",
    )(k_flat, e_flat, halves)


def apply_kernel(q_ref, c_ref, scale_ref, o_ref, ssq_ref):
    groups = c_ref.shape[1]
    width = q_ref.shape[1] // groups
    tokens = q_ref.shape[0]
    squares = jnp.zeros((tokens, 128), jnp.float32)
    for group in range(groups):
        q_part = q_ref[:, group * width : (group + 1) * width]
        c_one, c_three, c_two = (c_ref[:, group, mat].reshape(width, width) for mat in range(3))
        q_one = dot(q_part, c_one, ((1,), (0,)))
        q_three = dot(q_part, c_three, ((1,), (0,)))
        half = 0.5 * q_one
        a_query = ((half * jnp.tanh(half) + half) * q_three).astype(jnp.bfloat16)
        o_part = dot(a_query, c_two, ((1,), (0,))).astype(jnp.bfloat16)
        o_ref[:, group * width : (group + 1) * width] = o_part
        wide = o_part.astype(jnp.float32)
        wide = wide * wide
        lanes = wide[:, :128]
        for col in range(1, width // 128):
            lanes = lanes + wide[:, col * 128 : (col + 1) * 128]
        squares = squares + lanes * (scale_ref[group] * scale_ref[group])
    ssq_ref[...] = jnp.sum(squares.T, axis=0, keepdims=True)


def apply(q_flat, fresh, scales):
    cap_rows, both = q_flat.shape
    steps = cap_rows // APPLY_ROWS
    tokens = pl.BlockSpec((APPLY_ROWS, both), lambda t: (t, 0))
    return pl.pallas_call(
        apply_kernel,
        grid=(steps,),
        in_specs=[
            tokens,
            pl.BlockSpec(memory_space=pltpu.VMEM),
            pl.BlockSpec(memory_space=pltpu.SMEM),
        ],
        out_specs=[tokens, pl.BlockSpec((1, APPLY_ROWS), lambda t: (0, t))],
        out_shape=[
            jax.ShapeDtypeStruct(q_flat.shape, jnp.bfloat16),
            jax.ShapeDtypeStruct((1, cap_rows), jnp.float32),
        ],
        compiler_params=params(APPLY_MIB),
        name="apply",
    )(q_flat, fresh, scales)


def finish_kernel(o_ref, ssq_ref, scale_ref, live_ref, out):
    tokens, both = o_ref.shape
    groups = scale_ref.shape[0]
    width = both // groups
    lanes = 128
    tiles = width // lanes
    side = 256
    span = side // (groups * tiles)
    total_sq = jnp.sum(ssq_ref[...], axis=0)
    factor = lax.rsqrt(total_sq * scale_ref[groups - 1, 1] + EPS)
    place = pl.program_id(0) * tokens + lax.broadcasted_iota(jnp.int32, (1, tokens), 1)
    factor = jnp.where(place < live_ref[0], factor, 0.0)
    factor = jnp.broadcast_to(factor, (lanes, tokens)).T
    columns = []
    for start in range(0, tokens, span):
        rows = slice(start, start + span)
        pieces = []
        for group in range(groups):
            for tile in range(tiles):
                col = group * width + tile * lanes
                part = o_ref[rows, col : col + lanes].astype(jnp.float32) * scale_ref[group, 0]
                pieces.append(part * factor[rows])
        columns.append(jnp.concatenate(pieces, axis=0).astype(jnp.bfloat16))
    row = lax.broadcasted_iota(jnp.int32, (side, side), 0)
    col = lax.broadcasted_iota(jnp.int32, (side, side), 1)
    token, tile, group = row // (groups * tiles), row % (groups * tiles) // groups, row % groups
    order = jnp.where(col == (group * tiles + tile) * span + token, 1.0, 0.0).astype(jnp.bfloat16)
    mixed = dot(order, jnp.concatenate(columns, axis=1), ((1,), (0,))).astype(jnp.bfloat16)
    for index in range(len(columns)):
        out[index * side : (index + 1) * side] = mixed[:, index * lanes : (index + 1) * lanes]


def finish(fast, total_sq, scales, own_count):
    cap_rows, both = fast.shape
    lanes = 128
    rows = FINISH_ROWS * both // lanes
    return pl.pallas_call(
        finish_kernel,
        grid=(cap_rows // FINISH_ROWS,),
        in_specs=[
            pl.BlockSpec((FINISH_ROWS, both), lambda t: (t, 0)),
            pl.BlockSpec((total_sq.shape[0], 1, FINISH_ROWS), lambda t: (0, 0, t)),
            pl.BlockSpec(memory_space=pltpu.SMEM),
            pl.BlockSpec(memory_space=pltpu.SMEM),
        ],
        out_specs=pl.BlockSpec((rows, lanes), lambda t: (t, 0)),
        out_shape=jax.ShapeDtypeStruct((cap_rows * both // lanes, lanes), jnp.bfloat16),
        compiler_params=params(FINISH_MIB),
        name="finish",
    )(fast, total_sq, scales, own_count)


def exchange(blocks):
    return lax.all_to_all(blocks, "seq", 0, 0, tiled=True)


def shards(
    queries, key_rows, value_rows, step_rates, live_counts, group_scales, w_first, w_third, w_second
):
    cap_rows, groups, feat_width = queries.shape
    seq_size = lax.axis_size("seq")
    root_total = jnp.sqrt(jnp.float32(cap_rows * seq_size))
    own_count = live_counts[lax.axis_index("seq")]
    live_mask = jnp.arange(cap_rows, dtype=jnp.int32) < own_count
    weights = (w_first, w_third, w_second)
    halves = exchange(spread(weights, seq_size))
    eta = step_rates.T.astype(jnp.float32) * live_mask.astype(jnp.float32)[:, None] / root_total
    err = (eta[:, :, None] * value_rows.astype(jnp.float32)).astype(jnp.bfloat16)
    flat = (cap_rows, groups * feat_width)
    sums = exchange(terms(key_rows.reshape(flat), err.reshape(flat), halves))
    fresh = exchange(renew(sums, weights))
    fast, partial_sq = apply(queries.reshape(flat), fresh, group_scales)
    total_sq = lax.all_gather(partial_sq, "heads", axis=0)
    share = jnp.full_like(group_scales, 1.0 / (groups * feat_width * lax.axis_size("heads")))
    ordered = finish(fast, total_sq, jnp.stack((group_scales, share), axis=1), own_count[None])
    ordered = ordered.reshape(cap_rows, feat_width // 128, groups, 128).transpose(0, 2, 1, 3)
    return ordered.reshape(queries.shape)


def solution(mesh):
    in_specs = (
        P("seq", "heads", None),
        P("seq", "heads", None),
        P("seq", "heads", None),
        P("heads", "seq"),
        P(),
        P("heads"),
        P("heads", "seq", None),
        P("heads", "seq", None),
        P("heads", "seq", None),
    )
    out_specs = P("seq", "heads", None)
    return jax.shard_map(shards, mesh=mesh, in_specs=in_specs, out_specs=out_specs, check_vma=False)
```

```python
import functools
import jax
import jax.numpy as jnp
from jax import lax
from jax.experimental import pallas as pl
from jax.experimental.pallas import tpu as pltpu
from jax.sharding import PartitionSpec as P

EPS = 1e-06
TERM_ROWS = 512
SPREAD_MIB = 60
TERMS_MIB = 46
APPLY_MIB = 44
FINISH_MIB = 40
APPLY_ROWS = 512
FINISH_ROWS = 1024


def params(mebibytes):
    return pltpu.CompilerParams(vmem_limit_bytes=mebibytes * 1024 * 1024)


def dot(a, b, dims):
    return lax.dot_general(a, b, (dims, ((), ())), preferred_element_type=jnp.float32)


def send_all(chunk, wide, sems):
    copies = [pltpu.make_async_copy(chunk, wide.at[peer], sems.at[peer]) for peer in range(wide.shape[0])]
    for copy in copies:
        copy.start()
    for copy in copies:
        copy.wait()


def spread_kernel(w_first, w_third, w_second, wide, chunk, sems):
    for mat, ref in enumerate((w_first, w_third, w_second)):
        chunk[:, mat] = ref[...].astype(jnp.bfloat16)
    send_all(chunk, wide, sems)


def spread(weights, peers):
    groups, rows, width = weights[0].shape
    return pl.pallas_call(
        spread_kernel,
        out_specs=pl.BlockSpec(memory_space=pl.ANY),
        out_shape=jax.ShapeDtypeStruct((peers, groups, 3, rows, width), jnp.bfloat16),
        scratch_shapes=[
            pltpu.VMEM((groups, 3, rows, width), jnp.bfloat16),
            pltpu.SemaphoreType.DMA((peers,)),
        ],
        compiler_params=params(SPREAD_MIB),
        name="spread",
    )(*weights)


def renew_kernel(blocks, w_first, w_third, w_second, wide, chunk, sems):
    groups = blocks.shape[1]
    for mat, ref in enumerate((w_first, w_third, w_second)):
        for group in range(groups):
            term = jnp.sum(blocks[:, group, mat].astype(jnp.float32), axis=0)
            start = ref[group]
            update = start + term
            norm_old = jnp.mean(start * start, axis=-1, keepdims=True) + EPS
            norm_new = jnp.mean(update * update, axis=-1, keepdims=True) + EPS
            fresh = update * (jnp.sqrt(norm_old) / jnp.sqrt(norm_new))
            chunk[group, mat] = fresh.astype(jnp.bfloat16)
    send_all(chunk, wide, sems)


def renew(blocks, weights):
    return pl.pallas_call(
        renew_kernel,
        out_specs=pl.BlockSpec(memory_space=pl.ANY),
        out_shape=jax.ShapeDtypeStruct(blocks.shape, jnp.bfloat16),
        scratch_shapes=[
            pltpu.VMEM(blocks.shape[1:], jnp.bfloat16),
            pltpu.SemaphoreType.DMA(blocks.shape[:1]),
        ],
        compiler_params=params(24),
        name="renew",
    )(blocks, *weights)


def arrivals(group, part, parts):
    if group == 0 and part == 0:
        return [0]
    if part == (1 if group == 0 else 0):
        return range(part, parts)
    return []


def terms_kernel(k_hbm, e_hbm, b_ref, out, k_ref, e_ref, d_ref, a_ref, k_sems, e_sems):
    groups = b_ref.shape[1]
    cap_rows = k_hbm.shape[0]
    width = k_hbm.shape[1] // groups
    block = out.shape[:1] + out.shape[3:]
    copies = {}
    for group in range(groups):
        cols = pl.ds(group * width, width)
        for part in range(cap_rows // TERM_ROWS):
            rows = pl.ds(part * TERM_ROWS, TERM_ROWS)
            copies[group, part] = (
                pltpu.make_async_copy(k_hbm.at[rows, cols], k_ref.at[group, rows], k_sems.at[group, part]),
                pltpu.make_async_copy(e_hbm.at[rows, cols], e_ref.at[group, rows], e_sems.at[group, part]),
            )
            for copy in copies[group, part]:
                copy.start()
    for group in range(groups):
        b_one, b_three, b_two = (b_ref[:, group, mat].reshape(width, width) for mat in range(3))
        for part in range(cap_rows // TERM_ROWS):
            for arrival in arrivals(group, part, cap_rows // TERM_ROWS):
                for copy in copies[group, arrival]:
                    copy.wait()
            rows = slice(part * TERM_ROWS, (part + 1) * TERM_ROWS)
            k_part, err = k_ref[group, rows], e_ref[group, rows]
            h_one = dot(k_part, b_one, ((1,), (0,)))
            h_three = dot(k_part, b_three, ((1,), (0,)))
            back = dot(err, b_two, ((1,), (1,)))
            half = 0.5 * h_one
            turn = jnp.tanh(half)
            gate = half * turn + half
            sig = 0.5 * turn + 0.5
            a_ref[rows] = (gate * h_three).astype(jnp.bfloat16)
            d_ref[rows, :width] = (back * h_three * (sig + gate * (1.0 - sig))).astype(jnp.bfloat16)
            d_ref[rows, width:] = (back * gate).astype(jnp.bfloat16)
        p_in = dot(k_ref[group], d_ref[...], ((0,), (0,)))
        out[:, group, 0] = p_in[:, :width].astype(jnp.bfloat16).reshape(block)
        out[:, group, 1] = p_in[:, width:].astype(jnp.bfloat16).reshape(block)
        p_out = dot(a_ref[...], e_ref[group], ((0,), (0,)))
        out[:, group, 2] = p_out.astype(jnp.bfloat16).reshape(block)


def terms(k_flat, e_flat, halves):
    cap_rows = k_flat.shape[0]
    groups, width = halves.shape[1], halves.shape[4]
    parts = cap_rows // TERM_ROWS
    return pl.pallas_call(
        terms_kernel,
        in_specs=[
            pl.BlockSpec(memory_space=pl.ANY),
            pl.BlockSpec(memory_space=pl.ANY),
            pl.BlockSpec(memory_space=pltpu.VMEM),
        ],
        out_specs=pl.BlockSpec(memory_space=pltpu.VMEM),
        out_shape=jax.ShapeDtypeStruct(halves.shape, jnp.bfloat16),
        scratch_shapes=[
            pltpu.VMEM((groups, cap_rows, width), jnp.bfloat16),
            pltpu.VMEM((groups, cap_rows, width), jnp.bfloat16),
            pltpu.VMEM((cap_rows, 2 * width), jnp.bfloat16),
            pltpu.VMEM((cap_rows, width), jnp.bfloat16),
            pltpu.SemaphoreType.DMA((groups, parts)),
            pltpu.SemaphoreType.DMA((groups, parts)),
        ],
        compiler_params=params(TERMS_MIB),
        name="terms",
    )(k_flat, e_flat, halves)


def apply_kernel(q_ref, c_ref, scale_ref, o_ref, ssq_ref):
    groups = c_ref.shape[1]
    width = q_ref.shape[1] // groups
    tokens = q_ref.shape[0]
    own_rows = pl.ds(pl.multiple_of(pl.program_id(0) * tokens, tokens), tokens)
    squares = jnp.zeros((tokens, 128), jnp.float32)
    for group in range(groups):
        q_part = q_ref[:, group * width : (group + 1) * width]
        c_one, c_three, c_two = (c_ref[:, group, mat].reshape(width, width) for mat in range(3))
        q_one = dot(q_part, c_one, ((1,), (0,)))
        q_three = dot(q_part, c_three, ((1,), (0,)))
        half = 0.5 * q_one
        a_query = ((half * jnp.tanh(half) + half) * q_three).astype(jnp.bfloat16)
        o_part = dot(a_query, c_two, ((1,), (0,))).astype(jnp.bfloat16)
        o_ref[own_rows, group * width : (group + 1) * width] = o_part
        wide = o_part.astype(jnp.float32)
        wide = wide * wide
        lanes = wide[:, :128]
        for col in range(1, width // 128):
            lanes = lanes + wide[:, col * 128 : (col + 1) * 128]
        squares = squares + lanes * (scale_ref[group] * scale_ref[group])
    ssq_ref[...] = jnp.sum(squares.T, axis=0, keepdims=True)


def apply(q_flat, fresh, scales):
    cap_rows, both = q_flat.shape
    steps = cap_rows // APPLY_ROWS
    tokens = pl.BlockSpec((APPLY_ROWS, both), lambda t: (t, 0))
    return pl.pallas_call(
        apply_kernel,
        grid=(steps,),
        in_specs=[
            tokens,
            pl.BlockSpec(memory_space=pltpu.VMEM),
            pl.BlockSpec(memory_space=pltpu.SMEM),
        ],
        out_specs=[
            pl.BlockSpec(memory_space=pltpu.VMEM),
            pl.BlockSpec((1, APPLY_ROWS), lambda t: (0, t)),
        ],
        out_shape=[
            jax.ShapeDtypeStruct(q_flat.shape, jnp.bfloat16),
            jax.ShapeDtypeStruct((1, cap_rows), jnp.float32),
        ],
        compiler_params=params(APPLY_MIB),
        name="apply",
    )(q_flat, fresh, scales)


def finish_kernel(o_ref, ssq_ref, scale_ref, live_ref, out):
    tokens, both = FINISH_ROWS, o_ref.shape[1]
    base = pl.multiple_of(pl.program_id(0) * tokens, tokens)
    groups = scale_ref.shape[0]
    width = both // groups
    lanes = 128
    tiles = width // lanes
    side = 256
    span = side // (groups * tiles)
    total_sq = jnp.sum(ssq_ref[...], axis=0)
    factor = lax.rsqrt(total_sq * scale_ref[groups - 1, 1] + EPS)
    place = pl.program_id(0) * tokens + lax.broadcasted_iota(jnp.int32, (1, tokens), 1)
    factor = jnp.where(place < live_ref[0], factor, 0.0)
    factor = jnp.broadcast_to(factor, (lanes, tokens)).T
    columns = []
    for start in range(0, tokens, span):
        rows = slice(start, start + span)
        pieces = []
        for group in range(groups):
            for tile in range(tiles):
                col = group * width + tile * lanes
                part = o_ref[pl.ds(base + start, span), col : col + lanes].astype(jnp.float32) * scale_ref[group, 0]
                pieces.append(part * factor[rows])
        columns.append(jnp.concatenate(pieces, axis=0).astype(jnp.bfloat16))
    row = lax.broadcasted_iota(jnp.int32, (side, side), 0)
    col = lax.broadcasted_iota(jnp.int32, (side, side), 1)
    token, tile, group = row // (groups * tiles), row % (groups * tiles) // groups, row % groups
    order = jnp.where(col == (group * tiles + tile) * span + token, 1.0, 0.0).astype(jnp.bfloat16)
    mixed = dot(order, jnp.concatenate(columns, axis=1), ((1,), (0,))).astype(jnp.bfloat16)
    for index in range(len(columns)):
        out[index * side : (index + 1) * side] = mixed[:, index * lanes : (index + 1) * lanes]


def finish(fast, total_sq, scales, own_count):
    cap_rows, both = fast.shape
    lanes = 128
    rows = FINISH_ROWS * both // lanes
    return pl.pallas_call(
        finish_kernel,
        grid=(cap_rows // FINISH_ROWS,),
        in_specs=[
            pl.BlockSpec(memory_space=pltpu.VMEM),
            pl.BlockSpec((total_sq.shape[0], 1, FINISH_ROWS), lambda t: (0, 0, t)),
            pl.BlockSpec(memory_space=pltpu.SMEM),
            pl.BlockSpec(memory_space=pltpu.SMEM),
        ],
        out_specs=pl.BlockSpec((rows, lanes), lambda t: (t, 0)),
        out_shape=jax.ShapeDtypeStruct((cap_rows * both // lanes, lanes), jnp.bfloat16),
        compiler_params=params(FINISH_MIB),
        name="finish",
    )(fast, total_sq, scales, own_count)


def exchange(blocks):
    return lax.all_to_all(blocks, "seq", 0, 0, tiled=True)


def shards(
    queries, key_rows, value_rows, step_rates, live_counts, group_scales, w_first, w_third, w_second
):
    cap_rows, groups, feat_width = queries.shape
    seq_size = lax.axis_size("seq")
    root_total = jnp.sqrt(jnp.float32(cap_rows * seq_size))
    own_count = live_counts[lax.axis_index("seq")]
    live_mask = jnp.arange(cap_rows, dtype=jnp.int32) < own_count
    weights = (w_first, w_third, w_second)
    halves = exchange(spread(weights, seq_size))
    eta = step_rates.T.astype(jnp.float32) * live_mask.astype(jnp.float32)[:, None] / root_total
    err = (eta[:, :, None] * value_rows.astype(jnp.float32)).astype(jnp.bfloat16)
    flat = (cap_rows, groups * feat_width)
    sums = exchange(terms(key_rows.reshape(flat), err.reshape(flat), halves))
    fresh = exchange(renew(sums, weights))
    fast, partial_sq = apply(queries.reshape(flat), fresh, group_scales)
    total_sq = lax.all_gather(partial_sq, "heads", axis=0)
    share = jnp.full_like(group_scales, 1.0 / (groups * feat_width * lax.axis_size("heads")))
    ordered = finish(fast, total_sq, jnp.stack((group_scales, share), axis=1), own_count[None])
    ordered = ordered.reshape(cap_rows, feat_width // 128, groups, 128).transpose(0, 2, 1, 3)
    return ordered.reshape(queries.shape)


def solution(mesh):
    in_specs = (
        P("seq", "heads", None),
        P("seq", "heads", None),
        P("seq", "heads", None),
        P("heads", "seq"),
        P(),
        P("heads"),
        P("heads", "seq", None),
        P("heads", "seq", None),
        P("heads", "seq", None),
    )
    out_specs = P("seq", "heads", None)
    return jax.shard_map(shards, mesh=mesh, in_specs=in_specs, out_specs=out_specs, check_vma=False)
```

```python
import functools
import jax
import jax.numpy as jnp
from jax import lax
from jax.experimental import pallas as pl
from jax.experimental.pallas import tpu as pltpu
from jax.sharding import PartitionSpec as P

EPS = 1e-06
TERM_ROWS = 512
SPREAD_MIB = 60
TERMS_MIB = 46
APPLY_MIB = 44
FINISH_MIB = 40
APPLY_ROWS = 512
FINISH_ROWS = 1024


def params(mebibytes):
    return pltpu.CompilerParams(vmem_limit_bytes=mebibytes * 1024 * 1024)


def dot(a, b, dims):
    return lax.dot_general(a, b, (dims, ((), ())), preferred_element_type=jnp.float32)


def send_all(chunk, wide, sems):
    copies = [pltpu.make_async_copy(chunk, wide.at[peer], sems.at[peer]) for peer in range(wide.shape[0])]
    for copy in copies:
        copy.start()
    for copy in copies:
        copy.wait()


def spread_kernel(w_first, w_third, w_second, wide, chunk, sems):
    for mat, ref in enumerate((w_first, w_third, w_second)):
        chunk[:, mat] = ref[...].astype(jnp.bfloat16)
    send_all(chunk, wide, sems)


def spread(weights, peers):
    groups, rows, width = weights[0].shape
    return pl.pallas_call(
        spread_kernel,
        out_specs=pl.BlockSpec(memory_space=pl.ANY),
        out_shape=jax.ShapeDtypeStruct((peers, groups, 3, rows, width), jnp.bfloat16),
        scratch_shapes=[
            pltpu.VMEM((groups, 3, rows, width), jnp.bfloat16),
            pltpu.SemaphoreType.DMA((peers,)),
        ],
        compiler_params=params(SPREAD_MIB),
        name="spread",
    )(*weights)


def renew_kernel(blocks, w_first, w_third, w_second, wide, chunk, sems):
    groups = blocks.shape[1]
    for mat, ref in enumerate((w_first, w_third, w_second)):
        for group in range(groups):
            term = jnp.sum(blocks[:, group, mat].astype(jnp.float32), axis=0)
            start = ref[group]
            update = start + term
            norm_old = jnp.mean(start * start, axis=-1, keepdims=True) + EPS
            norm_new = jnp.mean(update * update, axis=-1, keepdims=True) + EPS
            fresh = update * (jnp.sqrt(norm_old) / jnp.sqrt(norm_new))
            chunk[group, mat] = fresh.astype(jnp.bfloat16)
    send_all(chunk, wide, sems)


def renew(blocks, weights):
    return pl.pallas_call(
        renew_kernel,
        out_specs=pl.BlockSpec(memory_space=pl.ANY),
        out_shape=jax.ShapeDtypeStruct(blocks.shape, jnp.bfloat16),
        scratch_shapes=[
            pltpu.VMEM(blocks.shape[1:], jnp.bfloat16),
            pltpu.SemaphoreType.DMA(blocks.shape[:1]),
        ],
        compiler_params=params(24),
        name="renew",
    )(blocks, *weights)


def arrivals(group, part, parts):
    if group == 0 and part == 0:
        return [0]
    if part == (1 if group == 0 else 0):
        return range(part, parts)
    return []


def terms_kernel(k_hbm, e_hbm, b_ref, out, k_ref, e_ref, d_ref, a_ref, k_sems, e_sems):
    groups = b_ref.shape[1]
    cap_rows = k_hbm.shape[0]
    width = k_hbm.shape[1] // groups
    block = out.shape[:1] + out.shape[3:]
    copies = {}
    for group in range(groups):
        cols = pl.ds(group * width, width)
        for part in range(cap_rows // TERM_ROWS):
            rows = pl.ds(part * TERM_ROWS, TERM_ROWS)
            copies[group, part] = (
                pltpu.make_async_copy(k_hbm.at[rows, cols], k_ref.at[group, rows], k_sems.at[group, part]),
                pltpu.make_async_copy(e_hbm.at[rows, cols], e_ref.at[group, rows], e_sems.at[group, part]),
            )
            for copy in copies[group, part]:
                copy.start()
    for group in range(groups):
        b_one, b_three, b_two = (b_ref[:, group, mat].reshape(width, width) for mat in range(3))
        for part in range(cap_rows // TERM_ROWS):
            for arrival in arrivals(group, part, cap_rows // TERM_ROWS):
                for copy in copies[group, arrival]:
                    copy.wait()
            rows = slice(part * TERM_ROWS, (part + 1) * TERM_ROWS)
            k_part, err = k_ref[group, rows], e_ref[group, rows]
            h_one = dot(k_part, b_one, ((1,), (0,)))
            h_three = dot(k_part, b_three, ((1,), (0,)))
            back = dot(err, b_two, ((1,), (1,)))
            half = 0.5 * h_one
            turn = jnp.tanh(half)
            gate = half * turn + half
            sig = 0.5 * turn + 0.5
            a_ref[rows] = (gate * h_three).astype(jnp.bfloat16)
            d_ref[rows, :width] = (back * h_three * (sig + gate * (1.0 - sig))).astype(jnp.bfloat16)
            d_ref[rows, width:] = (back * gate).astype(jnp.bfloat16)
        p_in = dot(k_ref[group], d_ref[...], ((0,), (0,)))
        out[:, group, 0] = p_in[:, :width].astype(jnp.bfloat16).reshape(block)
        out[:, group, 1] = p_in[:, width:].astype(jnp.bfloat16).reshape(block)
        p_out = dot(a_ref[...], e_ref[group], ((0,), (0,)))
        out[:, group, 2] = p_out.astype(jnp.bfloat16).reshape(block)


def terms(k_flat, e_flat, halves):
    cap_rows = k_flat.shape[0]
    groups, width = halves.shape[1], halves.shape[4]
    parts = cap_rows // TERM_ROWS
    return pl.pallas_call(
        terms_kernel,
        in_specs=[
            pl.BlockSpec(memory_space=pl.ANY),
            pl.BlockSpec(memory_space=pl.ANY),
            pl.BlockSpec(memory_space=pltpu.VMEM),
        ],
        out_specs=pl.BlockSpec(memory_space=pltpu.VMEM),
        out_shape=jax.ShapeDtypeStruct(halves.shape, jnp.bfloat16),
        scratch_shapes=[
            pltpu.VMEM((groups, cap_rows, width), jnp.bfloat16),
            pltpu.VMEM((groups, cap_rows, width), jnp.bfloat16),
            pltpu.VMEM((cap_rows, 2 * width), jnp.bfloat16),
            pltpu.VMEM((cap_rows, width), jnp.bfloat16),
            pltpu.SemaphoreType.DMA((groups, parts)),
            pltpu.SemaphoreType.DMA((groups, parts)),
        ],
        compiler_params=params(TERMS_MIB),
        name="terms",
    )(k_flat, e_flat, halves)


def apply_kernel(q_ref, c_ref, scale_ref, o_ref, ssq_ref):
    groups = c_ref.shape[1]
    width = q_ref.shape[1] // groups
    tokens = q_ref.shape[0]
    own_rows = pl.ds(pl.multiple_of(pl.program_id(0) * tokens, tokens), tokens)
    squares = jnp.zeros((tokens, 128), jnp.float32)
    for group in range(groups):
        q_part = q_ref[:, group * width : (group + 1) * width]
        c_one, c_three, c_two = (c_ref[:, group, mat].reshape(width, width) for mat in range(3))
        q_one = dot(q_part, c_one, ((1,), (0,)))
        q_three = dot(q_part, c_three, ((1,), (0,)))
        half = 0.5 * q_one
        a_query = ((half * jnp.tanh(half) + half) * q_three).astype(jnp.bfloat16)
        o_part = dot(a_query, c_two, ((1,), (0,))).astype(jnp.bfloat16)
        o_ref[own_rows, group * width : (group + 1) * width] = o_part
        wide = o_part.astype(jnp.float32)
        wide = wide * wide
        lanes = wide[:, :128]
        for col in range(1, width // 128):
            lanes = lanes + wide[:, col * 128 : (col + 1) * 128]
        squares = squares + lanes * (scale_ref[group] * scale_ref[group])
    ssq_ref[...] = jnp.sum(squares.T, axis=0, keepdims=True)


def apply(q_flat, fresh, scales):
    cap_rows, both = q_flat.shape
    steps = cap_rows // APPLY_ROWS
    tokens = pl.BlockSpec((APPLY_ROWS, both), lambda t: (t, 0))
    return pl.pallas_call(
        apply_kernel,
        grid=(steps,),
        in_specs=[
            tokens,
            pl.BlockSpec(memory_space=pltpu.VMEM),
            pl.BlockSpec(memory_space=pltpu.SMEM),
        ],
        out_specs=[
            pl.BlockSpec(memory_space=pltpu.VMEM),
            pl.BlockSpec((1, APPLY_ROWS), lambda t: (0, t)),
        ],
        out_shape=[
            jax.ShapeDtypeStruct(q_flat.shape, jnp.bfloat16),
            jax.ShapeDtypeStruct((1, cap_rows), jnp.float32),
        ],
        compiler_params=params(APPLY_MIB),
        name="apply",
    )(q_flat, fresh, scales)


def finish_kernel(share, o_ref, ssq_ref, scale_ref, live_ref, out):
    tokens, both = FINISH_ROWS, o_ref.shape[1]
    base = pl.multiple_of(pl.program_id(0) * tokens, tokens)
    groups = scale_ref.shape[0]
    width = both // groups
    lanes = 128
    tiles = width // lanes
    side = 256
    span = side // (groups * tiles)
    total_sq = jnp.sum(ssq_ref[...], axis=0)
    factor = lax.rsqrt(total_sq * share + EPS)
    place = pl.program_id(0) * tokens + lax.broadcasted_iota(jnp.int32, (1, tokens), 1)
    factor = jnp.where(place < live_ref[0], factor, 0.0)
    factor = jnp.broadcast_to(factor, (lanes, tokens)).T
    columns = []
    for start in range(0, tokens, span):
        rows = slice(start, start + span)
        pieces = []
        for group in range(groups):
            for tile in range(tiles):
                col = group * width + tile * lanes
                part = o_ref[pl.ds(base + start, span), col : col + lanes].astype(jnp.float32) * scale_ref[group]
                pieces.append(part * factor[rows])
        columns.append(jnp.concatenate(pieces, axis=0).astype(jnp.bfloat16))
    row = lax.broadcasted_iota(jnp.int32, (side, side), 0)
    col = lax.broadcasted_iota(jnp.int32, (side, side), 1)
    token, tile, group = row // (groups * tiles), row % (groups * tiles) // groups, row % groups
    order = jnp.where(col == (group * tiles + tile) * span + token, 1.0, 0.0).astype(jnp.bfloat16)
    mixed = dot(order, jnp.concatenate(columns, axis=1), ((1,), (0,))).astype(jnp.bfloat16)
    for index in range(len(columns)):
        out[index * side : (index + 1) * side] = mixed[:, index * lanes : (index + 1) * lanes]


def finish(fast, total_sq, scales, own_count, share):
    cap_rows, both = fast.shape
    lanes = 128
    rows = FINISH_ROWS * both // lanes
    return pl.pallas_call(
        functools.partial(finish_kernel, share),
        grid=(cap_rows // FINISH_ROWS,),
        in_specs=[
            pl.BlockSpec(memory_space=pltpu.VMEM),
            pl.BlockSpec((total_sq.shape[0], 1, FINISH_ROWS), lambda t: (0, 0, t)),
            pl.BlockSpec(memory_space=pltpu.SMEM),
            pl.BlockSpec(memory_space=pltpu.SMEM),
        ],
        out_specs=pl.BlockSpec((rows, lanes), lambda t: (t, 0)),
        out_shape=jax.ShapeDtypeStruct((cap_rows * both // lanes, lanes), jnp.bfloat16),
        compiler_params=params(FINISH_MIB),
        name="finish",
    )(fast, total_sq, scales, own_count)


def exchange(blocks):
    return lax.all_to_all(blocks, "seq", 0, 0, tiled=True)


def shards(
    queries, key_rows, value_rows, step_rates, live_counts, group_scales, w_first, w_third, w_second
):
    cap_rows, groups, feat_width = queries.shape
    seq_size = lax.axis_size("seq")
    root_total = jnp.sqrt(jnp.float32(cap_rows * seq_size))
    own_count = live_counts[lax.axis_index("seq")]
    live_mask = jnp.arange(cap_rows, dtype=jnp.int32) < own_count
    weights = (w_first, w_third, w_second)
    halves = exchange(spread(weights, seq_size))
    eta = step_rates.T.astype(jnp.float32) * live_mask.astype(jnp.float32)[:, None] / root_total
    err = (eta[:, :, None] * value_rows.astype(jnp.float32)).astype(jnp.bfloat16)
    flat = (cap_rows, groups * feat_width)
    q_flat, halves = lax.optimization_barrier((queries.reshape(flat), halves))
    sums = exchange(terms(key_rows.reshape(flat), err.reshape(flat), halves))
    fresh = exchange(renew(sums, weights))
    fast, partial_sq = apply(q_flat, fresh, group_scales)
    total_sq = lax.all_gather(partial_sq, "heads", axis=0)
    share = 1.0 / (groups * feat_width * lax.axis_size("heads"))
    ordered = finish(fast, total_sq, group_scales, own_count[None], share)
    ordered = ordered.reshape(cap_rows, feat_width // 128, groups, 128).transpose(0, 2, 1, 3)
    return ordered.reshape(queries.shape)


def solution(mesh):
    in_specs = (
        P("seq", "heads", None),
        P("seq", "heads", None),
        P("seq", "heads", None),
        P("heads", "seq"),
        P(),
        P("heads"),
        P("heads", "seq", None),
        P("heads", "seq", None),
        P("heads", "seq", None),
    )
    out_specs = P("seq", "heads", None)
    return jax.shard_map(shards, mesh=mesh, in_specs=in_specs, out_specs=out_specs, check_vma=False)
```

```python
import functools
import jax
import jax.numpy as jnp
from jax import lax
from jax.experimental import pallas as pl
from jax.experimental.pallas import tpu as pltpu
from jax.sharding import PartitionSpec as P

EPS = 1e-06
TERM_ROWS = 512
SPREAD_MIB = 60
TERMS_MIB = 46
APPLY_MIB = 44
FINISH_MIB = 40
APPLY_ROWS = 512
FINISH_ROWS = 1024


def params(mebibytes):
    return pltpu.CompilerParams(vmem_limit_bytes=mebibytes * 1024 * 1024)


def dot(a, b, dims):
    return lax.dot_general(a, b, (dims, ((), ())), preferred_element_type=jnp.float32)


def send_all(chunk, wide, sems):
    copies = [pltpu.make_async_copy(chunk, wide.at[peer], sems.at[peer]) for peer in range(wide.shape[0])]
    for copy in copies:
        copy.start()
    for copy in copies:
        copy.wait()


def spread_kernel(w_first, w_third, w_second, wide, chunk, sems):
    for mat, ref in enumerate((w_first, w_third, w_second)):
        chunk[:, mat] = ref[...].astype(jnp.bfloat16)
    send_all(chunk, wide, sems)


def spread(weights, peers):
    groups, rows, width = weights[0].shape
    return pl.pallas_call(
        spread_kernel,
        out_specs=pl.BlockSpec(memory_space=pl.ANY),
        out_shape=jax.ShapeDtypeStruct((peers, groups, 3, rows, width), jnp.bfloat16),
        scratch_shapes=[
            pltpu.VMEM((groups, 3, rows, width), jnp.bfloat16),
            pltpu.SemaphoreType.DMA((peers,)),
        ],
        compiler_params=params(SPREAD_MIB),
        name="spread",
    )(*weights)


def renew_kernel(blocks, w_first, w_third, w_second, wide):
    peers, groups = blocks.shape[:2]
    for mat, ref in enumerate((w_first, w_third, w_second)):
        for group in range(groups):
            term = jnp.sum(blocks[:, group, mat].astype(jnp.float32), axis=0)
            start = ref[group]
            update = start + term
            norm_old = jnp.mean(start * start, axis=-1, keepdims=True) + EPS
            norm_new = jnp.mean(update * update, axis=-1, keepdims=True) + EPS
            fresh = (update * (jnp.sqrt(norm_old) / jnp.sqrt(norm_new))).astype(jnp.bfloat16)
            for peer in range(peers):
                wide[peer, group, mat] = fresh


def renew(blocks, weights):
    return pl.pallas_call(
        renew_kernel,
        out_specs=pl.BlockSpec(memory_space=pltpu.VMEM),
        out_shape=jax.ShapeDtypeStruct(blocks.shape, jnp.bfloat16),
        compiler_params=params(24),
        name="renew",
    )(blocks, *weights)


def arrivals(group, part, parts):
    if group == 0 and part == 0:
        return [0]
    if part == (1 if group == 0 else 0):
        return range(part, parts)
    return []


def terms_kernel(k_hbm, e_hbm, b_ref, out, k_ref, e_ref, d_ref, a_ref, k_sems, e_sems):
    groups = b_ref.shape[1]
    cap_rows = k_hbm.shape[0]
    width = k_hbm.shape[1] // groups
    block = out.shape[:1] + out.shape[3:]
    copies = {}
    for group in range(groups):
        cols = pl.ds(group * width, width)
        for part in range(cap_rows // TERM_ROWS):
            rows = pl.ds(part * TERM_ROWS, TERM_ROWS)
            copies[group, part] = (
                pltpu.make_async_copy(k_hbm.at[rows, cols], k_ref.at[group, rows], k_sems.at[group, part]),
                pltpu.make_async_copy(e_hbm.at[rows, cols], e_ref.at[group, rows], e_sems.at[group, part]),
            )
            for copy in copies[group, part]:
                copy.start()
    for group in range(groups):
        b_one, b_three, b_two = (b_ref[:, group, mat].reshape(width, width) for mat in range(3))
        for part in range(cap_rows // TERM_ROWS):
            for arrival in arrivals(group, part, cap_rows // TERM_ROWS):
                for copy in copies[group, arrival]:
                    copy.wait()
            rows = slice(part * TERM_ROWS, (part + 1) * TERM_ROWS)
            k_part, err = k_ref[group, rows], e_ref[group, rows]
            h_one = dot(k_part, b_one, ((1,), (0,)))
            h_three = dot(k_part, b_three, ((1,), (0,)))
            back = dot(err, b_two, ((1,), (1,)))
            half = 0.5 * h_one
            turn = jnp.tanh(half)
            gate = half * turn + half
            sig = 0.5 * turn + 0.5
            a_ref[rows] = (gate * h_three).astype(jnp.bfloat16)
            d_ref[rows, :width] = (back * h_three * (sig + gate * (1.0 - sig))).astype(jnp.bfloat16)
            d_ref[rows, width:] = (back * gate).astype(jnp.bfloat16)
        p_in = dot(k_ref[group], d_ref[...], ((0,), (0,)))
        out[:, group, 0] = p_in[:, :width].astype(jnp.bfloat16).reshape(block)
        out[:, group, 1] = p_in[:, width:].astype(jnp.bfloat16).reshape(block)
        p_out = dot(a_ref[...], e_ref[group], ((0,), (0,)))
        out[:, group, 2] = p_out.astype(jnp.bfloat16).reshape(block)


def terms(k_flat, e_flat, halves):
    cap_rows = k_flat.shape[0]
    groups, width = halves.shape[1], halves.shape[4]
    parts = cap_rows // TERM_ROWS
    return pl.pallas_call(
        terms_kernel,
        in_specs=[
            pl.BlockSpec(memory_space=pl.ANY),
            pl.BlockSpec(memory_space=pl.ANY),
            pl.BlockSpec(memory_space=pltpu.VMEM),
        ],
        out_specs=pl.BlockSpec(memory_space=pltpu.VMEM),
        out_shape=jax.ShapeDtypeStruct(halves.shape, jnp.bfloat16),
        scratch_shapes=[
            pltpu.VMEM((groups, cap_rows, width), jnp.bfloat16),
            pltpu.VMEM((groups, cap_rows, width), jnp.bfloat16),
            pltpu.VMEM((cap_rows, 2 * width), jnp.bfloat16),
            pltpu.VMEM((cap_rows, width), jnp.bfloat16),
            pltpu.SemaphoreType.DMA((groups, parts)),
            pltpu.SemaphoreType.DMA((groups, parts)),
        ],
        compiler_params=params(TERMS_MIB),
        name="terms",
    )(k_flat, e_flat, halves)


def apply_kernel(q_ref, c_ref, scale_ref, o_ref, ssq_ref):
    groups = c_ref.shape[1]
    width = q_ref.shape[1] // groups
    tokens = q_ref.shape[0]
    own_rows = pl.ds(pl.multiple_of(pl.program_id(0) * tokens, tokens), tokens)
    squares = jnp.zeros((tokens, 128), jnp.float32)
    for group in range(groups):
        q_part = q_ref[:, group * width : (group + 1) * width]
        c_one, c_three, c_two = (c_ref[:, group, mat].reshape(width, width) for mat in range(3))
        q_one = dot(q_part, c_one, ((1,), (0,)))
        q_three = dot(q_part, c_three, ((1,), (0,)))
        half = 0.5 * q_one
        a_query = ((half * jnp.tanh(half) + half) * q_three).astype(jnp.bfloat16)
        o_part = dot(a_query, c_two, ((1,), (0,))).astype(jnp.bfloat16)
        o_ref[own_rows, group * width : (group + 1) * width] = o_part
        wide = o_part.astype(jnp.float32)
        wide = wide * wide
        lanes = wide[:, :128]
        for col in range(1, width // 128):
            lanes = lanes + wide[:, col * 128 : (col + 1) * 128]
        squares = squares + lanes * (scale_ref[group] * scale_ref[group])
    ssq_ref[...] = jnp.sum(squares.T, axis=0, keepdims=True)


def apply(q_flat, fresh, scales):
    cap_rows, both = q_flat.shape
    steps = cap_rows // APPLY_ROWS
    tokens = pl.BlockSpec((APPLY_ROWS, both), lambda t: (t, 0))
    return pl.pallas_call(
        apply_kernel,
        grid=(steps,),
        in_specs=[
            tokens,
            pl.BlockSpec(memory_space=pltpu.VMEM),
            pl.BlockSpec(memory_space=pltpu.SMEM),
        ],
        out_specs=[
            pl.BlockSpec(memory_space=pltpu.VMEM),
            pl.BlockSpec((1, APPLY_ROWS), lambda t: (0, t)),
        ],
        out_shape=[
            jax.ShapeDtypeStruct(q_flat.shape, jnp.bfloat16),
            jax.ShapeDtypeStruct((1, cap_rows), jnp.float32),
        ],
        compiler_params=params(APPLY_MIB),
        name="apply",
    )(q_flat, fresh, scales)


def finish_kernel(share, o_ref, ssq_ref, scale_ref, live_ref, out):
    tokens, both = FINISH_ROWS, o_ref.shape[1]
    base = pl.multiple_of(pl.program_id(0) * tokens, tokens)
    groups = scale_ref.shape[0]
    width = both // groups
    lanes = 128
    tiles = width // lanes
    side = 256
    span = side // (groups * tiles)
    total_sq = jnp.sum(ssq_ref[...], axis=0)
    factor = lax.rsqrt(total_sq * share + EPS)
    place = pl.program_id(0) * tokens + lax.broadcasted_iota(jnp.int32, (1, tokens), 1)
    factor = jnp.where(place < live_ref[0], factor, 0.0)
    factor = jnp.broadcast_to(factor, (lanes, tokens)).T
    columns = []
    for start in range(0, tokens, span):
        rows = slice(start, start + span)
        pieces = []
        for group in range(groups):
            for tile in range(tiles):
                col = group * width + tile * lanes
                part = o_ref[pl.ds(base + start, span), col : col + lanes].astype(jnp.float32) * scale_ref[group]
                pieces.append(part * factor[rows])
        columns.append(jnp.concatenate(pieces, axis=0).astype(jnp.bfloat16))
    row = lax.broadcasted_iota(jnp.int32, (side, side), 0)
    col = lax.broadcasted_iota(jnp.int32, (side, side), 1)
    token, tile, group = row // (groups * tiles), row % (groups * tiles) // groups, row % groups
    order = jnp.where(col == (group * tiles + tile) * span + token, 1.0, 0.0).astype(jnp.bfloat16)
    mixed = dot(order, jnp.concatenate(columns, axis=1), ((1,), (0,))).astype(jnp.bfloat16)
    for index in range(len(columns)):
        out[index * side : (index + 1) * side] = mixed[:, index * lanes : (index + 1) * lanes]


def finish(fast, total_sq, scales, own_count, share):
    cap_rows, both = fast.shape
    lanes = 128
    rows = FINISH_ROWS * both // lanes
    return pl.pallas_call(
        functools.partial(finish_kernel, share),
        grid=(cap_rows // FINISH_ROWS,),
        in_specs=[
            pl.BlockSpec(memory_space=pltpu.VMEM),
            pl.BlockSpec((total_sq.shape[0], 1, FINISH_ROWS), lambda t: (0, 0, t)),
            pl.BlockSpec(memory_space=pltpu.SMEM),
            pl.BlockSpec(memory_space=pltpu.SMEM),
        ],
        out_specs=pl.BlockSpec((rows, lanes), lambda t: (t, 0)),
        out_shape=jax.ShapeDtypeStruct((cap_rows * both // lanes, lanes), jnp.bfloat16),
        compiler_params=params(FINISH_MIB),
        name="finish",
    )(fast, total_sq, scales, own_count)


def exchange(blocks):
    return lax.all_to_all(blocks, "seq", 0, 0, tiled=True)


def shards(
    queries, key_rows, value_rows, step_rates, live_counts, group_scales, w_first, w_third, w_second
):
    cap_rows, groups, feat_width = queries.shape
    seq_size = lax.axis_size("seq")
    root_total = jnp.sqrt(jnp.float32(cap_rows * seq_size))
    own_count = live_counts[lax.axis_index("seq")]
    live_mask = jnp.arange(cap_rows, dtype=jnp.int32) < own_count
    weights = (w_first, w_third, w_second)
    halves = exchange(spread(weights, seq_size))
    eta = step_rates.T.astype(jnp.float32) * live_mask.astype(jnp.float32)[:, None] / root_total
    err = (eta[:, :, None] * value_rows.astype(jnp.float32)).astype(jnp.bfloat16)
    flat = (cap_rows, groups * feat_width)
    q_flat, halves = lax.optimization_barrier((queries.reshape(flat), halves))
    sums = exchange(terms(key_rows.reshape(flat), err.reshape(flat), halves))
    fresh = exchange(renew(sums, weights))
    fast, partial_sq = apply(q_flat, fresh, group_scales)
    total_sq = lax.all_gather(partial_sq, "heads", axis=0)
    share = 1.0 / (groups * feat_width * lax.axis_size("heads"))
    ordered = finish(fast, total_sq, group_scales, own_count[None], share)
    ordered = ordered.reshape(cap_rows, feat_width // 128, groups, 128).transpose(0, 2, 1, 3)
    return ordered.reshape(queries.shape)


def solution(mesh):
    in_specs = (
        P("seq", "heads", None),
        P("seq", "heads", None),
        P("seq", "heads", None),
        P("heads", "seq"),
        P(),
        P("heads"),
        P("heads", "seq", None),
        P("heads", "seq", None),
        P("heads", "seq", None),
    )
    out_specs = P("seq", "heads", None)
    return jax.shard_map(shards, mesh=mesh, in_specs=in_specs, out_specs=out_specs, check_vma=False)
```
